32 devices in a mesh: dp: 4 (over y, x), ctx: 8 (over z, core).
Axes of the slice: x: 2, y: 2, z: 4, core: 2. Of those that a mesh axis runs over, the one named last changes fastest.
Arguments:
- queries: bfloat16 [8192, 512], P(('dp', 'ctx')), parts along dimension 0, may hold values from -60 to 60
- keys: bfloat16 [8192, 512], P(('dp', 'ctx')), parts along dimension 0, may hold values from -6 to 6
- values: bfloat16 [8192, 512], P(('dp', 'ctx')), parts along dimension 0, may hold values from -6 to 6
- grad_out: bfloat16 [8192, 512], P(('dp', 'ctx')), parts along dimension 0, may hold values from -6 to 6
- window: int32 [4], replicated, may hold values from 128 to 256, as said below
- offsets: int32 [128, 4], P(('dp', 'ctx')), parts along dimension 0, may hold values from 5 to 67, as said below
Outputs:
- attended: bfloat16 [8192, 512], P(('dp', 'ctx')), parts along dimension 0
- grad_queries: bfloat16 [8192, 512], P(('dp', 'ctx')), parts along dimension 0
- grad_keys: bfloat16 [8192, 512], P(('dp', 'ctx')), parts along dimension 0
- grad_values: bfloat16 [8192, 512], P(('dp', 'ctx')), parts along dimension 0
The draws below stay inside these ranges and needn't reach their ends.
There are 4 independent parts, one for each index of `dp`. The reference program is written for one: setup_inputs(seed, part) draws one part's arguments, and reference() takes and returns one part's arrays. A program takes and returns all parts, laid end to end along the dimension named above; an argument that names none is the same for every part. Nothing has to cross between parts.
Inputs may be any that keep to these rules, and one draw needn't show every extreme that they name: `window`: every entry is between 128 and 256; some head has exactly 256 and some exactly 128. offsets[b, j] = 2 ** (j + 1) * 4 + (b % 4) - c with 0 <= c < 4, so the key block b - offsets[b, j] lies among the blocks of group b // 4 - 2 ** (j + 1).
All inputs are finite; a program needn't handle non-finite values.
Results may differ from the reference program's by a relative error of at most 0.017.
Values may be sent and summed in bfloat16 or wider, within the bound.
A program may use at most 64 MiB of HBM per device.

```python
import jax
import jax.numpy as jnp
from jax import lax

HEADS = 4
HEAD_DIM = 128
FEAT = 512
TOK_DEV = 256
BLOCK = 64
LEVELS = 4
DOC_LEN = 2048
DOC_BLOCKS = 32
DEV_BLOCKS = 4
N_CTX = 8


def paired_rows(key):
    base = jax.random.fold_in(key, 7)
    key_a, key_b = jax.random.split(base, 2)
    row_total = DOC_LEN
    width = HEADS * HEAD_DIM
    key_rows = jnp.clip(jax.random.normal(key_a, (row_total, width), jnp.float32), -6.0, 6.0)
    query_rows = jnp.clip(2.0 * jax.random.normal(key_b, (row_total, width), jnp.float32), -12.0, 12.0)
    return (query_rows, key_rows)


def draw_queries(key, part):
    return paired_rows(key)[0].astype(jnp.bfloat16)


def draw_keys(key, part):
    return paired_rows(key)[1].astype(jnp.bfloat16)


def draw_window(key, part):
    key_a, key_b = jax.random.split(jax.random.fold_in(key, 3))
    lengths = jax.random.randint(key_a, (HEADS,), TOK_DEV // 2, TOK_DEV + 1)
    widest = jax.random.randint(key_b, (), 0, HEADS)
    heads_idx = jnp.arange(HEADS, dtype=jnp.int32)
    lengths = jnp.where(heads_idx == widest, TOK_DEV, lengths)
    lengths = jnp.where(heads_idx == (widest + 1) % HEADS, TOK_DEV // 2, lengths)
    return lengths.astype(jnp.int32)


def draw_offsets(key, part):
    jitter = jax.random.randint(jax.random.fold_in(key, 11), (DOC_BLOCKS, LEVELS), 0, DEV_BLOCKS)
    jitter = jitter.at[0, 0].set(DEV_BLOCKS - 1)
    jitter = jitter.at[DOC_BLOCKS - 1, LEVELS - 1].set(0)
    rows = jnp.arange(DOC_BLOCKS, dtype=jnp.int32)
    base = 2 ** (jnp.arange(LEVELS, dtype=jnp.int32) + 1) * DEV_BLOCKS
    return (base[None, :] + (rows % DEV_BLOCKS)[:, None] - jitter).astype(jnp.int32)


def block_levels(stream_key, shape, pieces, least, largest):
    gain, own = 1.0, jax.random.fold_in(stream_key, 6)
    for dim, parts in pieces:
        heights = jnp.exp(jax.random.uniform(jax.random.fold_in(own, dim), (parts,), jnp.float32, least / len(pieces), largest / len(pieces)))
        gain = gain * jnp.repeat(heights, shape[dim] // parts).reshape([-1 if axis == dim else 1 for axis in range(len(shape))])
    return gain


def scatter_about(stream_key, dims, scale, limit, cuts=(), kind=jnp.bfloat16):
    values = scale * jax.random.normal(stream_key, dims, jnp.float32)
    if cuts:
        values = values * block_levels(stream_key, dims, cuts, -0.22, 0.18)
    return jnp.clip(values, -limit, limit).astype(kind)


def setup_inputs(seed: int = 0, part: int = 0) -> dict:
    arg_keys = jax.random.split(jax.random.key(seed), 7)
    part_keys = jax.random.split(jax.random.fold_in(arg_keys[6], part), 7)
    return {
        "queries": draw_queries(jax.random.fold_in(jax.random.fold_in(arg_keys[6], part), 71), part),
        "keys": draw_keys(jax.random.fold_in(jax.random.fold_in(arg_keys[6], part), 71), part),
        "values": scatter_about(part_keys[2], (DOC_LEN, FEAT), 1.0, 6.0, ((0, 8),)),
        "grad_out": scatter_about(part_keys[3], (DOC_LEN, FEAT), 1.0, 6.0, ((0, 8),)),
        "window": draw_window(jax.random.fold_in(arg_keys[6], 71), part),
        "offsets": draw_offsets(jax.random.fold_in(jax.random.fold_in(arg_keys[6], part), 71), part),
    }


def local_pass(rank_index, query_rows, key_prev, key_own, value_prev, value_own, level_keys, level_values, grad_rows, window, offset_rows):
    row_count, feat_count = query_rows.shape
    head_count = window.shape[0]
    head_size = feat_count // head_count
    block_count = row_count // BLOCK
    score_scale = head_size ** -0.5
    query_pos = rank_index * row_count + jnp.arange(row_count, dtype=jnp.int32)
    key_pos = rank_index * row_count - row_count + jnp.arange(2 * row_count, dtype=jnp.int32)
    query_heads = query_rows.astype(jnp.float32).reshape(row_count, head_count, head_size)
    query_blocks = query_heads.reshape(block_count, BLOCK, head_count, head_size)
    grad_heads = grad_rows.astype(jnp.float32).reshape(row_count, head_count, head_size)
    grad_blocks = grad_heads.reshape(block_count, BLOCK, head_count, head_size)
    win_keys = jnp.concatenate([key_prev, key_own], 0).astype(jnp.float32).reshape(2 * row_count, head_count, head_size)
    win_values = jnp.concatenate([value_prev, value_own], 0).astype(jnp.float32).reshape(2 * row_count, head_count, head_size)
    block_ids = rank_index * block_count + jnp.arange(block_count, dtype=jnp.int32)
    picked_keys = []
    picked_values = []
    level_ok = []
    block_index = []
    for depth_index in range(LEVELS):
        source = rank_index - 2 ** (depth_index + 1)
        inside = jnp.clip(block_ids - offset_rows[:, depth_index] - source * block_count, 0, block_count - 1).astype(jnp.int32)
        block_index.append(inside)
        picked_keys.append(level_keys[depth_index].reshape(block_count, BLOCK, feat_count)[inside])
        picked_values.append(level_values[depth_index].reshape(block_count, BLOCK, feat_count)[inside])
        level_ok.append(jnp.broadcast_to(source >= 0, (BLOCK,)))
    log_width = LEVELS * BLOCK
    log_keys = jnp.stack(picked_keys, 1).astype(jnp.float32).reshape(block_count, log_width, head_count, head_size)
    log_values = jnp.stack(picked_values, 1).astype(jnp.float32).reshape(block_count, log_width, head_count, head_size)
    log_allowed = jnp.concatenate(level_ok, 0)
    win_scores = jnp.einsum('qhd,khd->hqk', query_heads, win_keys) * score_scale
    log_scores = jnp.einsum('pqhd,pkhd->hpqk', query_blocks, log_keys).reshape(head_count, row_count, log_width) * score_scale
    win_allowed = (key_pos[None, None, :] <= query_pos[None, :, None]) & (key_pos[None, None, :] > query_pos[None, :, None] - window[:, None, None]) & (key_pos[None, None, :] >= 0)
    allowed = jnp.concatenate([win_allowed, jnp.broadcast_to(log_allowed[None, None, :], (head_count, row_count, log_width))], -1)
    scores = jnp.where(allowed, jnp.concatenate([win_scores, log_scores], -1), jnp.float32(-1e30))
    top = jnp.max(scores, -1)
    weights = jnp.exp(scores - top[..., None])
    total = jnp.sum(weights, -1)
    weights_low = weights.astype(jnp.bfloat16).astype(jnp.float32)
    split_at = 2 * row_count
    out_win = jnp.einsum('hqk,khd->qhd', weights_low[..., :split_at], win_values)
    out_log = jnp.einsum('hpqk,pkhd->pqhd', weights_low[..., split_at:].reshape(head_count, block_count, BLOCK, log_width), log_values).reshape(row_count, head_count, head_size)
    attended = ((out_win + out_log) / total.T[:, :, None]).astype(jnp.bfloat16)
    lse = top + jnp.log(total)
    probs = jnp.exp(scores - lse[..., None])
    probs_low = probs.astype(jnp.bfloat16).astype(jnp.float32)
    delta = jnp.sum(grad_heads * attended.astype(jnp.float32), -1).T
    dprob_win = jnp.einsum('qhd,khd->hqk', grad_heads, win_values)
    dprob_log = jnp.einsum('pqhd,pkhd->hpqk', grad_blocks, log_values).reshape(head_count, row_count, log_width)
    dscore = probs * (jnp.concatenate([dprob_win, dprob_log], -1) - delta[..., None])
    dscore_low = dscore.astype(jnp.bfloat16).astype(jnp.float32)
    dscore_win = dscore_low[..., :split_at]
    dscore_log = dscore_low[..., split_at:].reshape(head_count, block_count, BLOCK, log_width)
    probs_win = probs_low[..., :split_at]
    probs_log = probs_low[..., split_at:].reshape(head_count, block_count, BLOCK, log_width)
    grad_q = (jnp.einsum('hqk,khd->qhd', dscore_win, win_keys) + jnp.einsum('hpqk,pkhd->pqhd', dscore_log, log_keys).reshape(row_count, head_count, head_size)) * score_scale
    grad_q = grad_q.astype(jnp.bfloat16).reshape(row_count, feat_count)
    dkey_win = (jnp.einsum('hqk,qhd->khd', dscore_win, query_heads) * score_scale).reshape(split_at, feat_count)
    dval_win = jnp.einsum('hqk,qhd->khd', probs_win, grad_heads).reshape(split_at, feat_count)
    dkey_log = (jnp.einsum('hpqk,pqhd->pkhd', dscore_log, query_blocks) * score_scale).reshape(block_count, LEVELS, BLOCK, feat_count)
    dval_log = jnp.einsum('hpqk,pqhd->pkhd', probs_log, grad_blocks).reshape(block_count, LEVELS, BLOCK, feat_count)
    level_dkey = []
    level_dval = []
    for depth_index in range(LEVELS):
        onehot = (block_index[depth_index][:, None] == jnp.arange(block_count, dtype=jnp.int32)[None, :]).astype(jnp.float32)
        level_dkey.append(jnp.einsum('pc,pkf->ckf', onehot, dkey_log[:, depth_index], precision=lax.Precision.HIGHEST).reshape(row_count, feat_count).astype(jnp.bfloat16))
        level_dval.append(jnp.einsum('pc,pkf->ckf', onehot, dval_log[:, depth_index], precision=lax.Precision.HIGHEST).reshape(row_count, feat_count).astype(jnp.bfloat16))
    return (attended.reshape(row_count, feat_count), grad_q, dkey_win[row_count:], dval_win[row_count:],
            dkey_win[:row_count].astype(jnp.bfloat16), dval_win[:row_count].astype(jnp.bfloat16),
            jnp.stack(level_dkey, 0), jnp.stack(level_dval, 0))


def shift_up(stacked, distance):
    if distance >= N_CTX:
        return jnp.zeros_like(stacked).astype(jnp.float32)
    tail = jnp.zeros((distance,) + stacked.shape[1:], jnp.float32)
    return jnp.concatenate([stacked[distance:].astype(jnp.float32), tail], 0)


def reference(queries, keys, values, grad_out, window, offsets):
    feat_count = queries.shape[1]
    row_count = TOK_DEV
    block_count = row_count // BLOCK
    margin = 2 ** LEVELS
    key_pad = jnp.concatenate([jnp.zeros((margin, row_count, feat_count), keys.dtype), keys.reshape(N_CTX, row_count, feat_count)], 0)
    value_pad = jnp.concatenate([jnp.zeros((margin, row_count, feat_count), values.dtype), values.reshape(N_CTX, row_count, feat_count)], 0)
    query_shards = queries.reshape(N_CTX, row_count, feat_count)
    grad_shards = grad_out.reshape(N_CTX, row_count, feat_count)

    def one_group(rank_index):
        pick = lambda table, back: lax.dynamic_index_in_dim(table, rank_index - back + margin, 0, keepdims=False)
        level_keys = [pick(key_pad, 2 ** (j + 1)) for j in range(LEVELS)]
        level_values = [pick(value_pad, 2 ** (j + 1)) for j in range(LEVELS)]
        offset_rows = lax.dynamic_slice_in_dim(offsets, (rank_index * block_count).astype(jnp.int32), block_count, 0)
        return local_pass(rank_index, query_shards[rank_index], pick(key_pad, 1), pick(key_pad, 0), pick(value_pad, 1), pick(value_pad, 0),
                          level_keys, level_values, grad_shards[rank_index], window, offset_rows)

    results = lax.map(one_group, jnp.arange(N_CTX, dtype=jnp.int32))
    attended, grad_q, own_dkey, own_dval, prev_dkey, prev_dval, lev_dkey, lev_dval = results
    grad_keys = own_dkey + shift_up(prev_dkey, 1)
    grad_values = own_dval + shift_up(prev_dval, 1)
    for j in range(LEVELS):
        grad_keys = grad_keys + shift_up(lev_dkey[:, j], 2 ** (j + 1))
        grad_values = grad_values + shift_up(lev_dval[:, j], 2 ** (j + 1))
    shape_out = (N_CTX * row_count, feat_count)
    return (attended.reshape(shape_out), grad_q.reshape(shape_out),
            grad_keys.astype(jnp.bfloat16).reshape(shape_out), grad_values.astype(jnp.bfloat16).reshape(shape_out))
```

```python
import functools
import math

import jax
import jax.numpy as jnp
from jax import lax
from jax.experimental import pallas as pl
from jax.experimental.pallas import tpu as pltpu
from jax.sharding import PartitionSpec as P

BLOCK = 64
LEVELS = 4
HEAD = 128
NEG = -1e30
MESH = pl.DeviceIdType.MESH
NT = (((1,), (1,)), ((), ()))
TN = (((0,), (0,)), ((), ()))
NN = (((1,), (0,)), ((), ()))


def dot(a, b, dims):
    return lax.dot_general(a, b, dims, preferred_element_type=jnp.float32)


def kernel(
    size, heads, far,
    window, offsets, q_ref, k_ref, v_ref, do_ref,
    att_ref, gq_ref, gk_ref, gv_ref,
    own, rx1, rx2, rx4, rxf,
    tg1, tg4, ts2, tgf, rg1, rg4, rs2, rgf, hold2, acc,
    send, recv,
):
    f32, bf16 = jnp.float32, jnp.bfloat16
    rows = q_ref.shape[0]
    r = lax.axis_index("ctx")
    odd = lax.rem(r, 2) == 1
    even = jnp.logical_not(odd)
    has_up = r + 2 < size
    scale = HEAD ** -0.5
    mate = r + 1 - 2 * lax.rem(r, 2)

    K_OWN, K_REL, K_PRV, K_G4, K_S2, K_G1, K_FAR = 0, 1, 2, 3, 4, 5, 6
    K_GFAR = K_FAR + len(far)

    def copy(kind, h, src, dst, to):
        return pltpu.make_async_remote_copy(
            src_ref=src, dst_ref=dst, send_sem=send.at[kind, h], recv_sem=recv.at[kind, h],
            device_id={"ctx": to}, device_id_type=MESH,
        )

    def own_up(h):
        return copy(K_OWN, h, own.at[h], rx2.at[h], r + 2)

    def relay_up(h):
        return copy(K_REL, h, rx2.at[h], rx4.at[h], r + 2)

    def prev_own(h):
        return copy(K_PRV, h, own.at[h], rx1.at[h], mate)

    def prev_relay(h):
        return copy(K_PRV, h, rx2.at[h], rx1.at[h], mate)

    def far_up(n, h):
        return copy(K_FAR + n, h, own.at[h], rxf.at[n, h], r + far[n])

    def g4_down(h):
        return copy(K_G4, h, tg4.at[h], rg4.at[h], r - 2)

    def s2_down(h):
        return copy(K_S2, h, ts2.at[h], rs2.at[h], r - 2)

    def g1_mate(h):
        return copy(K_G1, h, tg1.at[h], rg1.at[h], mate)

    def gfar_down(n, h):
        return copy(K_GFAR + n, h, tgf.at[n, h], rgf.at[n, h], r - far[n])

    barrier = pltpu.get_barrier_semaphore()
    pl.semaphore_signal(barrier, inc=1, device_id={"ctx": mate}, device_id_type=MESH)
    count = 1
    for d in (2,) + far:
        for to, ok in ((r + d, r + d < size), (r - d, r >= d)):
            count = count + ok.astype(jnp.int32)

            @pl.when(ok)
            def _(to=to):
                pl.semaphore_signal(barrier, inc=1, device_id={"ctx": to}, device_id_type=MESH)

    for h in range(heads):
        cols = slice(h * HEAD, (h + 1) * HEAD)
        own[h, 0] = k_ref[:, cols]
        own[h, 1] = v_ref[:, cols]
    for d, buf in ((1, rx1), (2, rx2), (4, rx4)):

        @pl.when(r < d)
        def _(buf=buf):
            buf[...] = jnp.zeros_like(buf)

    for n, d in enumerate(far):

        @pl.when(r < d)
        def _(n=n):
            rxf[n] = jnp.zeros(rxf.shape[1:], bf16)

    pl.semaphore_wait(barrier, count)

    def start_own(h):
        @pl.when(has_up)
        def _():
            own_up(h).start()

        for n in range(len(far)):

            @pl.when(r + far[n] < size)
            def _(n=n):
                far_up(n, h).start()

    start_own(0)
    start_own(1)

    @pl.when(even)
    def _():
        for h in range(heads):
            prev_own(h).start()

    key_i = lax.broadcasted_iota(jnp.int32, (rows, rows), 0)
    query_i = lax.broadcasted_iota(jnp.int32, (rows, rows), 1)
    diff = key_i - query_i
    tri = diff <= 0
    key_block = key_i // BLOCK
    query_block = lax.broadcasted_iota(jnp.int32, (1, rows), 1) // BLOCK
    dists = (2, 4) + far
    picks = []
    for j, d in enumerate(dists):
        pick = jnp.zeros((1, rows), jnp.int32)
        for p in range(rows // BLOCK):
            inside = p + d * (rows // BLOCK) - offsets[p, j]
            pick = jnp.where(query_block == p, inside, pick)
        picks.append(jnp.where(r >= d, pick, -1))

    def compute(h):
        cols = slice(h * HEAD, (h + 1) * HEAD)
        q = q_ref[:, cols]
        do = do_ref[:, cols]
        sources = [own[h], rx1[h], rx2[h], rx4[h]] + [rxf[n, h] for n in range(len(far))]
        ks = [x[0] for x in sources]
        vs = [x[1] for x in sources]
        w = window[h]
        limit = jnp.where(r >= 1, rows - w, 2 * rows)
        ok_win = (tri & (diff > -w)) | (diff > limit)
        raw = [dot(k, q, NT) for k in ks]
        scores = [jnp.where(ok_win, jnp.where(tri, raw[0], raw[1]), NEG)]
        for pick, s in zip(picks, raw[2:]):
            scores.append(jnp.where(key_block == pick, s, NEG))
        top = functools.reduce(jnp.maximum, [jnp.max(s, 0, keepdims=True) for s in scores])
        c = scale * math.log2(math.e)
        weights = [jnp.exp2((s - top) * c) for s in scores]
        total = functools.reduce(jnp.add, [jnp.sum(x, 0, keepdims=True) for x in weights])
        inv = 1.0 / total
        probs = [x * inv for x in weights]

        def spread(parts):
            first = parts[0]
            cut = [jnp.where(tri, first, 0.0), jnp.where(tri, 0.0, first)] + parts[1:]
            return [x.astype(bf16) for x in cut]

        p_low = spread(probs)
        v_all = jnp.concatenate(vs, 0)
        out_t = dot(v_all, jnp.concatenate(p_low, 0), TN)
        att = out_t.T.astype(bf16)
        att_ref[:, cols] = att
        delta = jnp.sum((att.astype(f32) * do.astype(f32)).T, 0, keepdims=True)
        raw = [dot(v, do, NT) for v in vs]
        dprobs = [jnp.where(tri, raw[0], raw[1])] + raw[2:]
        ds = spread([p * (x - delta) for p, x in zip(probs, dprobs)])
        gq = dot(jnp.concatenate(ks, 0), jnp.concatenate(ds, 0), TN) * scale
        gq_ref[:, cols] = gq.T.astype(bf16)
        dk = [dot(x, q, NN) * scale for x in ds]
        dv = [dot(x, do, NN) for x in p_low]
        acc[h, 0] = dk[0]
        acc[h, 1] = dv[0]
        tg1[h, 0] = dk[1].astype(bf16)
        tg1[h, 1] = dv[1].astype(bf16)
        hold2[h, 0] = dk[2]
        hold2[h, 1] = dv[2]
        tg4[h, 0] = dk[3].astype(bf16)
        tg4[h, 1] = dv[3].astype(bf16)
        for n in range(len(far)):
            tgf[n, h, 0] = dk[4 + n].astype(bf16)
            tgf[n, h, 1] = dv[4 + n].astype(bf16)

        @pl.when(r >= 4)
        def _():
            g4_down(h).start()

        @pl.when(r >= 1)
        def _():
            g1_mate(h).start()

        for n in range(len(far)):

            @pl.when(r >= far[n])
            def _(n=n):
                gfar_down(n, h).start()

    def combine(h):
        @pl.when((r >= 2) & has_up)
        def _():
            g4_down(h).wait_recv()
            hold2[h] = hold2[h] + rg4[h].astype(f32)

        @pl.when(odd & (r >= 3))
        def _():
            g1_mate(h).wait_recv()
            hold2[h] = hold2[h] + rg1[h].astype(f32)

        @pl.when(r >= 2)
        def _():
            ts2[h] = hold2[h].astype(bf16)
            s2_down(h).start()

    for i in range(heads + 1):
        if i < heads:

            @pl.when(r >= 2)
            def _(i=i):
                own_up(i).wait_recv()

            @pl.when((r >= 2) & has_up)
            def _(i=i):
                relay_up(i).start()

            @pl.when(odd & (r >= 3))
            def _(i=i):
                prev_relay(i).start()

            if i + 2 < heads:
                start_own(i + 2)
        if i >= 1:
            h = i - 1

            @pl.when(r >= 1)
            def _(h=h):
                prev_own(h).wait_recv()

            @pl.when(r >= 4)
            def _(h=h):
                relay_up(h).wait_recv()

            for n in range(len(far)):

                @pl.when(r >= far[n])
                def _(n=n, h=h):
                    far_up(n, h).wait_recv()

            compute(h)
        if i >= 2:
            combine(i - 2)
    combine(heads - 1)

    for h in range(heads):
        cols = slice(h * HEAD, (h + 1) * HEAD)

        @pl.when(even)
        def _(h=h):
            g1_mate(h).wait_recv()
            acc[h] = acc[h] + rg1[h].astype(f32)

        for n in range(len(far)):

            @pl.when(r + far[n] < size)
            def _(n=n, h=h):
                gfar_down(n, h).wait_recv()
                acc[h] = acc[h] + rgf[n, h].astype(f32)

        @pl.when(has_up)
        def _(h=h):
            s2_down(h).wait_recv()
            acc[h] = acc[h] + rs2[h].astype(f32)

        gk_ref[:, cols] = acc[h, 0].astype(bf16)
        gv_ref[:, cols] = acc[h, 1].astype(bf16)

    for h in range(heads):

        @pl.when(has_up)
        def _(h=h):
            own_up(h).wait_send()

        @pl.when((r >= 2) & has_up)
        def _(h=h):
            relay_up(h).wait_send()

        @pl.when(even | (r >= 3))
        def _(h=h):
            prev_own(h).wait_send()

        @pl.when(r >= 4)
        def _(h=h):
            g4_down(h).wait_send()

        @pl.when(r >= 2)
        def _(h=h):
            s2_down(h).wait_send()

        @pl.when(r >= 1)
        def _(h=h):
            g1_mate(h).wait_send()

        for n in range(len(far)):

            @pl.when(r + far[n] < size)
            def _(n=n, h=h):
                far_up(n, h).wait_send()

            @pl.when(r >= far[n])
            def _(n=n, h=h):
                gfar_down(n, h).wait_send()


def on_device(queries, keys, values, grad_out, window, offsets):
    size = lax.axis_size("ctx")
    rows, feat = queries.shape
    heads = feat // HEAD
    far = tuple(2 ** (j + 1) for j in range(2, LEVELS) if 2 ** (j + 1) < size)
    nf = max(len(far), 1)
    kinds = 6 + 2 * len(far)
    vmem = pl.BlockSpec(memory_space=pltpu.VMEM)
    smem = pl.BlockSpec(memory_space=pltpu.SMEM)
    pack = (heads, 2, rows, HEAD)
    small = pltpu.VMEM(pack, jnp.bfloat16)
    wide = pltpu.VMEM(pack, jnp.float32)
    more = pltpu.VMEM((nf,) + (pack if far else (1, 2, 16, HEAD)), jnp.bfloat16)
    out = jax.ShapeDtypeStruct((rows, feat), jnp.bfloat16)
    return pl.pallas_call(
        functools.partial(kernel, size, heads, far),
        out_shape=(out,) * 4,
        in_specs=[smem, smem] + [vmem] * 4,
        out_specs=(vmem,) * 4,
        scratch_shapes=[small] * 4 + [more] + [small] * 3 + [more] + [small] * 3 + [more]
        + [wide] * 2
        + [pltpu.SemaphoreType.DMA((kinds, heads)), pltpu.SemaphoreType.DMA((kinds, heads))],
        compiler_params=pltpu.CompilerParams(
            collective_id=0, has_side_effects=True, vmem_limit_bytes=48 * 2**20
        ),
        cost_estimate=pl.CostEstimate(
            flops=12 * heads * rows * rows * HEAD * (4 + len(far)),
            bytes_accessed=16 * rows * feat,
            transcendentals=heads * rows * rows * (3 + len(far)),
        ),
    )(window, offsets, queries, keys, values, grad_out)


def solution(mesh):
    cut = P(("dp", "ctx"), None)
    return jax.shard_map(
        on_device,
        mesh=mesh,
        in_specs=(cut, cut, cut, cut, P(), cut),
        out_specs=(cut,) * 4,
        check_vma=False,
    )
```

```python
import functools
import math

import jax
import jax.numpy as jnp
from jax import lax
from jax.experimental import pallas as pl
from jax.experimental.pallas import tpu as pltpu
from jax.sharding import PartitionSpec as P

BLOCK = 64
LEVELS = 4
HEAD = 128
NEG = -1e30
MESH = pl.DeviceIdType.MESH
NT = (((1,), (1,)), ((), ()))
TN = (((0,), (0,)), ((), ()))
NN = (((1,), (0,)), ((), ()))


def dot(a, b, dims):
    return lax.dot_general(a, b, dims, preferred_element_type=jnp.float32)


def kernel(
    size, heads, far,
    window_hbm, offsets_hbm, q_hbm, k_hbm, v_hbm, do_hbm,
    att_ref, gq_ref, gk_ref, gv_ref,
    window, offsets, q_ref, do_ref, tri_low, own, rx1, rx2, rx4, rxf,
    tg1, tg4, ts2, tgf, rg1, rg4, rs2, rgf, hold2, acc,
    send, recv, load, load_small,
):
    f32, bf16 = jnp.float32, jnp.bfloat16
    rows = q_hbm.shape[0]
    r = lax.axis_index("ctx")
    odd = lax.rem(r, 2) == 1
    even = jnp.logical_not(odd)
    has_up = r + 2 < size
    scale = HEAD ** -0.5
    mate = r + 1 - 2 * lax.rem(r, 2)

    K_OWN, K_REL, K_PRV, K_G4, K_S2, K_G1, K_FAR = 0, 1, 2, 3, 4, 5, 6
    K_GFAR = K_FAR + len(far)

    def copy(kind, h, src, dst, to):
        return pltpu.make_async_remote_copy(
            src_ref=src, dst_ref=dst, send_sem=send.at[kind, h], recv_sem=recv.at[kind, h],
            device_id={"ctx": to}, device_id_type=MESH,
        )

    def own_up(h):
        return copy(K_OWN, h, own.at[h], rx2.at[h], r + 2)

    def relay_up(h):
        return copy(K_REL, h, rx2.at[h], rx4.at[h], r + 2)

    def prev_own(h):
        return copy(K_PRV, h, own.at[h], rx1.at[h], mate)

    def prev_relay(h):
        return copy(K_PRV, h, rx2.at[h], rx1.at[h], mate)

    def far_up(n, h):
        return copy(K_FAR + n, h, own.at[h], rxf.at[n, h], r + far[n])

    def g4_down(h):
        return copy(K_G4, h, tg4.at[h], rg4.at[h], r - 2)

    def s2_down(h):
        return copy(K_S2, h, ts2.at[h], rs2.at[h], r - 2)

    def g1_mate(h):
        return copy(K_G1, h, tg1.at[h], rg1.at[h], mate)

    def gfar_down(n, h):
        return copy(K_GFAR + n, h, tgf.at[n, h], rgf.at[n, h], r - far[n])

    loads = []
    for h in range(heads):
        cols = slice(h * HEAD, (h + 1) * HEAD)
        loads.append([
            pltpu.make_async_copy(src.at[:, cols], dst, load.at[h, n])
            for n, (src, dst) in enumerate((
                (k_hbm, own.at[h, 0]), (v_hbm, own.at[h, 1]),
                (q_hbm, q_ref.at[h]), (do_hbm, do_ref.at[h]),
            ))
        ])
    small_copies = [
        pltpu.make_async_copy(offsets_hbm, offsets, load_small.at[0]),
        pltpu.make_async_copy(window_hbm, window, load_small.at[1]),
    ]
    for pair in (slice(0, 2), slice(2, 4)):
        for group in loads:
            for c in group[pair]:
                c.start()
    for c in small_copies:
        c.start()

    barrier = pltpu.get_barrier_semaphore()
    pl.semaphore_signal(barrier, inc=1, device_id={"ctx": mate}, device_id_type=MESH)
    count = 1
    for d in (2,) + far:
        for to, ok in ((r + d, r + d < size), (r - d, r >= d)):
            count = count + ok.astype(jnp.int32)

            @pl.when(ok)
            def _(to=to):
                pl.semaphore_signal(barrier, inc=1, device_id={"ctx": to}, device_id_type=MESH)

    for d, buf in ((1, rx1), (2, rx2), (4, rx4)):

        @pl.when(r < d)
        def _(buf=buf):
            buf[...] = jnp.zeros_like(buf)

    for n, d in enumerate(far):

        @pl.when(r < d)
        def _(n=n):
            rxf[n] = jnp.zeros(rxf.shape[1:], bf16)

    pl.semaphore_wait(barrier, count)

    def start_own(h):
        @pl.when(has_up)
        def _():
            own_up(h).start()

        for n in range(len(far)):

            @pl.when(r + far[n] < size)
            def _(n=n):
                far_up(n, h).start()

    def loaded(h):
        for c in loads[h][:2]:
            c.wait()

    loaded(0)
    start_own(0)
    loaded(1)
    start_own(1)
    for h in range(2, heads):
        loaded(h)

    @pl.when(even)
    def _():
        for h in range(heads):
            prev_own(h).start()

    for group in loads:
        for c in group[2:]:
            c.wait()

    query_i = lax.broadcasted_iota(jnp.int32, (rows, rows), 0)
    key_i = lax.broadcasted_iota(jnp.int32, (rows, rows), 1)
    diff = key_i - query_i
    tri = diff <= 0
    tri_low[0] = jnp.where(tri, 1.0, 0.0).astype(bf16)
    tri_low[1] = jnp.where(diff >= 0, 1.0, 0.0).astype(bf16)
    dists = (2, 4) + far
    wide_log = len(dists) * BLOCK
    lane = lax.broadcasted_iota(jnp.int32, (1, wide_log), 1) // BLOCK
    log_ok = functools.reduce(
        jnp.logical_or, [(lane == j) & (r >= d) for j, d in enumerate(dists)]
    )
    groups = rows // BLOCK
    for c in small_copies:
        c.wait()
    one_row = lax.broadcasted_iota(jnp.int32, (1, HEAD), 1) * 0
    chosen = [
        [
            [
                jnp.where(one_row + (p + d * groups - offsets[p, j]) == place, 1.0, 0.0)
                for place in range(groups)
            ]
            for j, d in enumerate(dists)
        ]
        for p in range(groups)
    ]
    chosen_low = [[[x.astype(bf16) for x in y] for y in z] for z in chosen]

    def block(x, p):
        return x[p * BLOCK:(p + 1) * BLOCK]

    def compute(h):
        cols = slice(h * HEAD, (h + 1) * HEAD)
        q = q_ref[h]
        do = do_ref[h]
        far_bufs = [rx2.at[h], rx4.at[h]] + [rxf.at[n, h] for n in range(len(far))]

        def picked(which):
            arrays = [buf[which] for buf in far_bufs[:len(dists)]]

            def pick(p, j):
                terms = [
                    block(arrays[j], place) * chosen_low[p][j][place] for place in range(groups)
                ]
                return functools.reduce(jnp.add, terms)

            return [
                jnp.concatenate([pick(p, j) for j in range(len(dists))], 0)
                for p in range(groups)
            ]

        k_own, k_prev, k_log = own[h, 0], rx1[h, 0], picked(0)
        v_own, v_prev, v_log = own[h, 1], rx1[h, 1], picked(1)

        def against(x, a, b, log):
            near = jnp.where(tri, dot(x, a, NT), dot(x, b, NT))
            return near, jnp.concatenate(
                [dot(block(x, p), log[p], NT) for p in range(groups)], 0
            )

        def weighted(xa, xb, xl, a, b, log):
            return dot(xa, a, NN) + dot(xb, b, NN) + jnp.concatenate(
                [dot(block(xl, p), log[p], NN) for p in range(groups)], 0
            )

        w = window[h]
        limit = jnp.where(r >= 1, rows - w, 2 * rows)
        ok_win = (tri & (diff > -w)) | (diff > limit)
        s_win, s_log = against(q, k_own, k_prev, k_log)
        s_win = jnp.where(ok_win, s_win, NEG)
        s_log = jnp.where(log_ok, s_log, NEG)
        top = jnp.maximum(jnp.max(s_win, 1, keepdims=True), jnp.max(s_log, 1, keepdims=True))
        c = scale * math.log2(math.e)
        w_win = jnp.exp2((s_win - top) * c)
        w_log = jnp.exp2((s_log - top) * c)
        inv = 1.0 / (jnp.sum(w_win, 1, keepdims=True) + jnp.sum(w_log, 1, keepdims=True))
        p_win = w_win * inv
        p_log = w_log * inv
        low = p_win.astype(bf16)
        low_own = low * tri_low[0]
        low_log = p_log.astype(bf16)
        att = weighted(low_own, low - low_own, low_log, v_own, v_prev, v_log).astype(bf16)
        att_ref[:, cols] = att

        def transposed(near, log, x):
            flip = near.T
            flip_own = flip * tri_low[1]
            return dot(flip_own, x, NN), dot(flip - flip_own, x, NN), [
                dot(block(log, p), block(x, p), TN) for p in range(groups)
            ]

        def scattered(parts, j):
            pieces = [block(x, j) for x in parts]
            return jnp.concatenate(
                [
                    functools.reduce(
                        jnp.add, [pieces[p] * chosen[p][j][place] for p in range(groups)]
                    )
                    for place in range(groups)
                ],
                0,
            )

        def keep(which, near, prev, log, factor):
            acc[h, which] = near * factor
            tg1[h, which] = (prev * factor).astype(bf16)
            hold2[h, which] = scattered(log, 0) * factor
            if len(dists) > 1:
                tg4[h, which] = (scattered(log, 1) * factor).astype(bf16)
            for n in range(len(far)):
                tgf[n, h, which] = (scattered(log, 2 + n) * factor).astype(bf16)

        keep(1, *transposed(low, low_log, do), 1.0)
        delta = jnp.sum(att.astype(f32) * do.astype(f32), 1, keepdims=True)
        d_win, d_log = against(do, v_own, v_prev, v_log)
        ds = (p_win * (d_win - delta)).astype(bf16)
        ds_own = ds * tri_low[0]
        ds_log = (p_log * (d_log - delta)).astype(bf16)
        gq = weighted(ds_own, ds - ds_own, ds_log, k_own, k_prev, k_log) * scale
        gq_ref[:, cols] = gq.astype(bf16)
        keep(0, *transposed(ds, ds_log, q), scale)

        @pl.when(r >= 4)
        def _():
            g4_down(h).start()

        @pl.when(r >= 1)
        def _():
            g1_mate(h).start()

        for n in range(len(far)):

            @pl.when(r >= far[n])
            def _(n=n):
                gfar_down(n, h).start()

    def combine(h):
        @pl.when((r >= 2) & has_up)
        def _():
            g4_down(h).wait_recv()
            hold2[h] = hold2[h] + rg4[h].astype(f32)

        @pl.when(odd & (r >= 3))
        def _():
            g1_mate(h).wait_recv()
            hold2[h] = hold2[h] + rg1[h].astype(f32)

        @pl.when(r >= 2)
        def _():
            ts2[h] = hold2[h].astype(bf16)
            s2_down(h).start()

    for i in range(heads + 1):
        if i < heads:

            @pl.when(r >= 2)
            def _(i=i):
                own_up(i).wait_recv()

            @pl.when((r >= 2) & has_up)
            def _(i=i):
                relay_up(i).start()

            @pl.when(odd & (r >= 3))
            def _(i=i):
                prev_relay(i).start()

            if i + 2 < heads:
                start_own(i + 2)
        if i >= 1:
            h = i - 1

            @pl.when(r >= 1)
            def _(h=h):
                prev_own(h).wait_recv()

            @pl.when(r >= 4)
            def _(h=h):
                relay_up(h).wait_recv()

            for n in range(len(far)):

                @pl.when(r >= far[n])
                def _(n=n, h=h):
                    far_up(n, h).wait_recv()

            compute(h)
        if i >= 2:
            combine(i - 2)
    combine(heads - 1)

    for h in range(heads):
        cols = slice(h * HEAD, (h + 1) * HEAD)

        @pl.when(even)
        def _(h=h):
            g1_mate(h).wait_recv()
            acc[h] = acc[h] + rg1[h].astype(f32)

        for n in range(len(far)):

            @pl.when(r + far[n] < size)
            def _(n=n, h=h):
                gfar_down(n, h).wait_recv()
                acc[h] = acc[h] + rgf[n, h].astype(f32)

        @pl.when(has_up)
        def _(h=h):
            s2_down(h).wait_recv()
            acc[h] = acc[h] + rs2[h].astype(f32)

        gk_ref[:, cols] = acc[h, 0].astype(bf16)
        gv_ref[:, cols] = acc[h, 1].astype(bf16)

    for h in range(heads):

        @pl.when(has_up)
        def _(h=h):
            own_up(h).wait_send()

        @pl.when((r >= 2) & has_up)
        def _(h=h):
            relay_up(h).wait_send()

        @pl.when(even | (r >= 3))
        def _(h=h):
            prev_own(h).wait_send()

        @pl.when(r >= 4)
        def _(h=h):
            g4_down(h).wait_send()

        @pl.when(r >= 2)
        def _(h=h):
            s2_down(h).wait_send()

        @pl.when(r >= 1)
        def _(h=h):
            g1_mate(h).wait_send()

        for n in range(len(far)):

            @pl.when(r + far[n] < size)
            def _(n=n, h=h):
                far_up(n, h).wait_send()

            @pl.when(r >= far[n])
            def _(n=n, h=h):
                gfar_down(n, h).wait_send()


def on_device(queries, keys, values, grad_out, window, offsets):
    size = lax.axis_size("ctx")
    rows, feat = queries.shape
    heads = feat // HEAD
    far = tuple(2 ** (j + 1) for j in range(2, LEVELS) if 2 ** (j + 1) < size)
    nf = max(len(far), 1)
    kinds = 6 + 2 * len(far)
    vmem = pl.BlockSpec(memory_space=pltpu.VMEM)
    hbm = pl.BlockSpec(memory_space=pltpu.HBM)
    pack = (heads, 2, rows, HEAD)
    small = pltpu.VMEM(pack, jnp.bfloat16)
    wide = pltpu.VMEM(pack, jnp.float32)
    more = pltpu.VMEM((nf,) + (pack if far else (1, 2, 16, HEAD)), jnp.bfloat16)
    out = jax.ShapeDtypeStruct((rows, feat), jnp.bfloat16)
    return pl.pallas_call(
        functools.partial(kernel, size, heads, far),
        out_shape=(out,) * 4,
        in_specs=[hbm] * 6,
        out_specs=(vmem,) * 4,
        scratch_shapes=[
            pltpu.SMEM(window.shape, jnp.int32),
            pltpu.SMEM(offsets.shape, jnp.int32),
            pltpu.VMEM((heads, rows, HEAD), jnp.bfloat16),
            pltpu.VMEM((heads, rows, HEAD), jnp.bfloat16),
            pltpu.VMEM((2, rows, rows), jnp.bfloat16),
        ]
        + [small] * 4 + [more] + [small] * 3 + [more] + [small] * 3 + [more]
        + [wide] * 2
        + [pltpu.SemaphoreType.DMA((kinds, heads)), pltpu.SemaphoreType.DMA((kinds, heads))]
        + [pltpu.SemaphoreType.DMA((heads, 4)), pltpu.SemaphoreType.DMA((2,))],
        compiler_params=pltpu.CompilerParams(
            collective_id=0, has_side_effects=True, vmem_limit_bytes=48 * 2**20
        ),
        cost_estimate=pl.CostEstimate(
            flops=12 * heads * rows * rows * HEAD * (4 + len(far)),
            bytes_accessed=16 * rows * feat,
            transcendentals=heads * rows * rows * (3 + len(far)),
        ),
    )(window, offsets, queries, keys, values, grad_out)


def solution(mesh):
    cut = P(("dp", "ctx"), None)
    return jax.shard_map(
        on_device,
        mesh=mesh,
        in_specs=(cut, cut, cut, cut, P(), cut),
        out_specs=(cut,) * 4,
        check_vma=False,
    )
```

```python
import functools
import math

import jax
import jax.numpy as jnp
from jax import lax
from jax.experimental import pallas as pl
from jax.experimental.pallas import tpu as pltpu
from jax.sharding import PartitionSpec as P

BLOCK = 64
LEVELS = 4
HEAD = 128
NEG = -1e30
AHEAD = 3
MESH = pl.DeviceIdType.MESH
NT = (((1,), (1,)), ((), ()))
TN = (((0,), (0,)), ((), ()))
NN = (((1,), (0,)), ((), ()))


def dot(a, b, dims):
    return lax.dot_general(a, b, dims, preferred_element_type=jnp.float32)


def kernel(
    size, heads, far,
    window_hbm, offsets_hbm, q_hbm, k_hbm, v_hbm, do_hbm,
    att_hbm, gq_hbm, gk_hbm, gv_hbm,
    staged, window, offsets, q_ref, do_ref, tri_low, own, rx1, rx2, rx4, rxf,
    tg1, tg4, ts2, tgf, rg1, rg4, rs2, rgf, hold2, acc,
    send, recv, load, load_small, store,
):
    f32, bf16 = jnp.float32, jnp.bfloat16
    rows = q_hbm.shape[0]
    r = lax.axis_index("ctx")
    odd = lax.rem(r, 2) == 1
    even = jnp.logical_not(odd)
    has_up = r + 2 < size
    scale = HEAD ** -0.5
    mate = r + 1 - 2 * lax.rem(r, 2)

    K_OWN, K_REL, K_PRV, K_G4, K_S2, K_G1, K_FAR = 0, 1, 2, 3, 4, 5, 6
    K_GFAR = K_FAR + len(far)

    def copy(kind, h, src, dst, to):
        return pltpu.make_async_remote_copy(
            src_ref=src, dst_ref=dst, send_sem=send.at[kind, h], recv_sem=recv.at[kind, h],
            device_id={"ctx": to}, device_id_type=MESH,
        )

    def piece(buf, i):
        return buf.at[i // 2, i % 2]

    def own_up(i):
        return copy(K_OWN, i, piece(own, i), piece(rx2, i), r + 2)

    def relay_up(i):
        return copy(K_REL, i, piece(rx2, i), piece(rx4, i), r + 2)

    def prev_own(i):
        return copy(K_PRV, i, piece(own, i), piece(rx1, i), mate)

    def prev_relay(i):
        return copy(K_PRV, i, piece(rx2, i), piece(rx1, i), mate)

    def far_up(n, i):
        return copy(K_FAR + n, i, piece(own, i), piece(rxf.at[n], i), r + far[n])

    def g4_down(i):
        return copy(K_G4, i, piece(tg4, i), piece(rg4, i), r - 2)

    def s2_down(i):
        return copy(K_S2, i, piece(ts2, i), piece(rs2, i), r - 2)

    def g1_mate(i):
        return copy(K_G1, i, piece(tg1, i), piece(rg1, i), mate)

    def gfar_down(n, i):
        return copy(K_GFAR + n, i, piece(tgf.at[n], i), piece(rgf.at[n], i), r - far[n])

    def result(n, h):
        out = (att_hbm, gq_hbm, gk_hbm, gv_hbm)[n]
        return pltpu.make_async_copy(
            staged.at[n, h], out.at[:, h * HEAD:(h + 1) * HEAD], store.at[n, h]
        )

    loads = []
    for h in range(heads):
        cols = slice(h * HEAD, (h + 1) * HEAD)
        loads.append([
            pltpu.make_async_copy(src.at[:, cols], dst, load.at[h, n])
            for n, (src, dst) in enumerate((
                (k_hbm, own.at[h, 0]), (v_hbm, own.at[h, 1]),
                (q_hbm, q_ref.at[h]), (do_hbm, do_ref.at[h]),
            ))
        ])
    small_copies = [
        pltpu.make_async_copy(offsets_hbm, offsets, load_small.at[0]),
        pltpu.make_async_copy(window_hbm, window, load_small.at[1]),
    ]
    for pair in (slice(0, 2), slice(2, 4)):
        for group in loads:
            for c in group[pair]:
                c.start()
    for c in small_copies:
        c.start()

    barrier = pltpu.get_barrier_semaphore()
    pl.semaphore_signal(barrier, inc=1, device_id={"ctx": mate}, device_id_type=MESH)
    count = 1
    for d in (2,) + far:
        for to, ok in ((r + d, r + d < size), (r - d, r >= d)):
            count = count + ok.astype(jnp.int32)

            @pl.when(ok)
            def _(to=to):
                pl.semaphore_signal(barrier, inc=1, device_id={"ctx": to}, device_id_type=MESH)

    for d, buf in ((1, rx1), (2, rx2), (4, rx4)):

        @pl.when(r < d)
        def _(buf=buf):
            buf[...] = jnp.zeros_like(buf)

    for n, d in enumerate(far):

        @pl.when(r < d)
        def _(n=n):
            rxf[n] = jnp.zeros(rxf.shape[1:], bf16)

    pl.semaphore_wait(barrier, count)

    pieces = 2 * heads

    def start_own(i):
        loads[i // 2][i % 2].wait()

        @pl.when(has_up)
        def _():
            own_up(i).start()

        @pl.when(even)
        def _():
            prev_own(i).start()

        for n in range(len(far)):

            @pl.when(r + far[n] < size)
            def _(n=n):
                far_up(n, i).start()

    for i in range(AHEAD):
        start_own(i)
    for group in loads:
        for c in group[2:]:
            c.wait()

    query_i = lax.broadcasted_iota(jnp.int32, (rows, rows), 0)
    key_i = lax.broadcasted_iota(jnp.int32, (rows, rows), 1)
    diff = key_i - query_i
    tri = diff <= 0
    tri_low[0] = jnp.where(tri, 1.0, 0.0).astype(bf16)
    tri_low[1] = jnp.where(diff >= 0, 1.0, 0.0).astype(bf16)
    dists = (2, 4) + far
    wide_log = len(dists) * BLOCK
    lane = lax.broadcasted_iota(jnp.int32, (1, wide_log), 1) // BLOCK
    log_ok = functools.reduce(
        jnp.logical_or, [(lane == j) & (r >= d) for j, d in enumerate(dists)]
    )
    groups = rows // BLOCK
    for c in small_copies:
        c.wait()
    one_row = lax.broadcasted_iota(jnp.int32, (1, HEAD), 1) * 0
    chosen = [
        [
            [
                jnp.where(one_row + (p + d * groups - offsets[p, j]) == place, 1.0, 0.0)
                for place in range(groups)
            ]
            for j, d in enumerate(dists)
        ]
        for p in range(groups)
    ]
    chosen_low = [[[x.astype(bf16) for x in y] for y in z] for z in chosen]

    def block(x, p):
        return x[p * BLOCK:(p + 1) * BLOCK]

    def send_back(i):
        @pl.when(r >= 4)
        def _():
            g4_down(i).start()

        @pl.when(r >= 1)
        def _():
            g1_mate(i).start()

        for n in range(len(far)):

            @pl.when(r >= far[n])
            def _(n=n):
                gfar_down(n, i).start()

    def compute(h):
        q = q_ref[h]
        do = do_ref[h]
        far_bufs = [rx2.at[h], rx4.at[h]] + [rxf.at[n, h] for n in range(len(far))]

        def picked(which):
            arrays = [buf[which] for buf in far_bufs[:len(dists)]]

            def pick(p, j):
                terms = [
                    block(arrays[j], place) * chosen_low[p][j][place] for place in range(groups)
                ]
                return functools.reduce(jnp.add, terms)

            return [
                jnp.concatenate([pick(p, j) for j in range(len(dists))], 0)
                for p in range(groups)
            ]

        arrive(2 * h)
        k_own, k_prev, k_log = own[h, 0], rx1[h, 0], picked(0)

        def against(x, a, b, log):
            near = jnp.where(tri, dot(x, a, NT), dot(x, b, NT))
            return near, jnp.concatenate(
                [dot(block(x, p), log[p], NT) for p in range(groups)], 0
            )

        def weighted(xa, xb, xl, a, b, log):
            return dot(xa, a, NN) + dot(xb, b, NN) + jnp.concatenate(
                [dot(block(xl, p), log[p], NN) for p in range(groups)], 0
            )

        w = window[h]
        limit = jnp.where(r >= 1, rows - w, 2 * rows)
        ok_win = (tri & (diff > -w)) | (diff > limit)
        s_win, s_log = against(q, k_own, k_prev, k_log)
        s_win = jnp.where(ok_win, s_win, NEG)
        s_log = jnp.where(log_ok, s_log, NEG)
        top = jnp.maximum(jnp.max(s_win, 1, keepdims=True), jnp.max(s_log, 1, keepdims=True))
        c = scale * math.log2(math.e)
        w_win = jnp.exp2((s_win - top) * c)
        w_log = jnp.exp2((s_log - top) * c)
        inv = 1.0 / (jnp.sum(w_win, 1, keepdims=True) + jnp.sum(w_log, 1, keepdims=True))
        p_win = w_win * inv
        p_log = w_log * inv
        low = p_win.astype(bf16)
        low_own = low * tri_low[0]
        low_log = p_log.astype(bf16)
        def transposed(near, log, x):
            flip = near.T
            flip_own = flip * tri_low[1]
            return dot(flip_own, x, NN), dot(flip - flip_own, x, NN), [
                dot(block(log, p), block(x, p), TN) for p in range(groups)
            ]

        def scattered(parts, j):
            pieces = [block(x, j) for x in parts]
            return jnp.concatenate(
                [
                    functools.reduce(
                        jnp.add, [pieces[p] * chosen[p][j][place] for p in range(groups)]
                    )
                    for place in range(groups)
                ],
                0,
            )

        def keep(which, near, prev, log, factor):
            acc[h, which] = near * factor
            tg1[h, which] = (prev * factor).astype(bf16)
            hold2[h, which] = scattered(log, 0) * factor
            if len(dists) > 1:
                tg4[h, which] = (scattered(log, 1) * factor).astype(bf16)
            for n in range(len(far)):
                tgf[n, h, which] = (scattered(log, 2 + n) * factor).astype(bf16)

        keep(1, *transposed(low, low_log, do), 1.0)
        send_back(2 * h + 1)
        yield
        arrive(2 * h + 1)
        v_own, v_prev, v_log = own[h, 1], rx1[h, 1], picked(1)
        att = weighted(low_own, low - low_own, low_log, v_own, v_prev, v_log).astype(bf16)
        staged[0, h] = att
        result(0, h).start()
        delta = jnp.sum(att.astype(f32) * do.astype(f32), 1, keepdims=True)
        d_win, d_log = against(do, v_own, v_prev, v_log)
        ds = (p_win * (d_win - delta)).astype(bf16)
        ds_own = ds * tri_low[0]
        ds_log = (p_log * (d_log - delta)).astype(bf16)
        keep(0, *transposed(ds, ds_log, q), scale)
        send_back(2 * h)
        gq = weighted(ds_own, ds - ds_own, ds_log, k_own, k_prev, k_log) * scale
        staged[1, h] = gq.astype(bf16)
        result(1, h).start()
        yield

    def combine(i):
        h, w = i // 2, i % 2

        @pl.when((r >= 2) & has_up)
        def _():
            g4_down(i).wait_recv()
            hold2[h, w] = hold2[h, w] + rg4[h, w].astype(f32)

        @pl.when(odd & (r >= 3))
        def _():
            g1_mate(i).wait_recv()
            hold2[h, w] = hold2[h, w] + rg1[h, w].astype(f32)

        @pl.when(r >= 2)
        def _():
            ts2[h, w] = hold2[h, w].astype(bf16)
            s2_down(i).start()

    def relay(i):
        @pl.when(r >= 2)
        def _():
            own_up(i).wait_recv()

        @pl.when((r >= 2) & has_up)
        def _():
            relay_up(i).start()

        @pl.when(odd & (r >= 3))
        def _():
            prev_relay(i).start()

        if i + AHEAD < pieces:
            start_own(i + AHEAD)

    def arrive(i):
        @pl.when(r >= 1)
        def _():
            prev_own(i).wait_recv()

        @pl.when(r >= 4)
        def _():
            relay_up(i).wait_recv()

        for n in range(len(far)):

            @pl.when(r >= far[n])
            def _(n=n):
                far_up(n, i).wait_recv()

    def finish(i):
        h, w = i // 2, i % 2

        @pl.when(even)
        def _():
            g1_mate(i).wait_recv()
            acc[h, w] = acc[h, w] + rg1[h, w].astype(f32)

        for n in range(len(far)):

            @pl.when(r + far[n] < size)
            def _(n=n):
                gfar_down(n, i).wait_recv()
                acc[h, w] = acc[h, w] + rgf[n, h, w].astype(f32)

        @pl.when(has_up)
        def _():
            s2_down(i).wait_recv()
            acc[h, w] = acc[h, w] + rs2[h, w].astype(f32)

        staged[2 + w, h] = acc[h, w].astype(bf16)
        result(2 + w, h).start()

    back = [i for h in range(heads) for i in (2 * h + 1, 2 * h)]
    steps = [compute(h) for h in range(heads)]
    for i in range(AHEAD):
        relay(i)
    for i in range(pieces):
        next(steps[i // 2])
        if i + AHEAD < pieces:
            relay(i + AHEAD)
        if i >= 1:
            combine(back[i - 1])
    combine(back[-1])
    for i in back:
        finish(i)

    for i in range(pieces):

        @pl.when(has_up)
        def _(i=i):
            own_up(i).wait_send()

        @pl.when((r >= 2) & has_up)
        def _(i=i):
            relay_up(i).wait_send()

        @pl.when(even | (r >= 3))
        def _(i=i):
            prev_own(i).wait_send()

        @pl.when(r >= 4)
        def _(i=i):
            g4_down(i).wait_send()

        @pl.when(r >= 2)
        def _(i=i):
            s2_down(i).wait_send()

        @pl.when(r >= 1)
        def _(i=i):
            g1_mate(i).wait_send()

        for n in range(len(far)):

            @pl.when(r + far[n] < size)
            def _(n=n, i=i):
                far_up(n, i).wait_send()

            @pl.when(r >= far[n])
            def _(n=n, i=i):
                gfar_down(n, i).wait_send()

    for n in range(4):
        for h in range(heads):
            result(n, h).wait()


def copy_out(*refs):
    sems = refs[-1]
    copies = [
        pltpu.make_async_copy(refs[n], refs[4 + n], sems.at[n]) for n in range(4)
    ]
    for c in copies:
        c.start()
    for c in copies:
        c.wait()


def on_device(queries, keys, values, grad_out, window, offsets):
    size = lax.axis_size("ctx")
    rows, feat = queries.shape
    heads = feat // HEAD
    far = tuple(2 ** (j + 1) for j in range(2, LEVELS) if 2 ** (j + 1) < size)
    nf = max(len(far), 1)
    kinds = 6 + 2 * len(far)
    hbm = pl.BlockSpec(memory_space=pltpu.HBM)
    pack = (heads, 2, rows, HEAD)
    small = pltpu.VMEM(pack, jnp.bfloat16)
    wide = pltpu.VMEM(pack, jnp.float32)
    more = pltpu.VMEM((nf,) + (pack if far else (1, 2, 16, HEAD)), jnp.bfloat16)
    out = jax.ShapeDtypeStruct((rows, feat), jnp.bfloat16)
    parts = pl.pallas_call(
        functools.partial(kernel, size, heads, far),
        out_shape=(out,) * 4,
        in_specs=[hbm] * 6,
        out_specs=(hbm,) * 4,
        scratch_shapes=[
            pltpu.VMEM((4, heads, rows, HEAD), jnp.bfloat16),
            pltpu.SMEM(window.shape, jnp.int32),
            pltpu.SMEM(offsets.shape, jnp.int32),
            pltpu.VMEM((heads, rows, HEAD), jnp.bfloat16),
            pltpu.VMEM((heads, rows, HEAD), jnp.bfloat16),
            pltpu.VMEM((2, rows, rows), jnp.bfloat16),
        ]
        + [small] * 4 + [more] + [small] * 3 + [more] + [small] * 3 + [more]
        + [wide] * 2
        + [pltpu.SemaphoreType.DMA((kinds, 2 * heads)), pltpu.SemaphoreType.DMA((kinds, 2 * heads))]
        + [pltpu.SemaphoreType.DMA((heads, 4)), pltpu.SemaphoreType.DMA((2,))]
        + [pltpu.SemaphoreType.DMA((4, heads))],
        compiler_params=pltpu.CompilerParams(
            collective_id=0, has_side_effects=True, vmem_limit_bytes=63 * 2**20
        ),
        cost_estimate=pl.CostEstimate(
            flops=12 * heads * rows * rows * HEAD * (4 + len(far)),
            bytes_accessed=16 * rows * feat,
            transcendentals=heads * rows * rows * (3 + len(far)),
        ),
    )(window, offsets, queries, keys, values, grad_out)
    return pl.pallas_call(
        copy_out,
        out_shape=(out,) * 4,
        in_specs=[hbm] * 4,
        out_specs=(hbm,) * 4,
        scratch_shapes=[pltpu.SemaphoreType.DMA((4,))],
        compiler_params=pltpu.CompilerParams(vmem_limit_bytes=63 * 2**20),
        cost_estimate=pl.CostEstimate(
            flops=0, bytes_accessed=16 * rows * feat, transcendentals=0
        ),
    )(*parts)


def solution(mesh):
    cut = P(("dp", "ctx"), None)
    return jax.shard_map(
        on_device,
        mesh=mesh,
        in_specs=(cut, cut, cut, cut, P(), cut),
        out_specs=(cut,) * 4,
        check_vma=False,
    )
```

```python
import functools
import math

import jax
import jax.numpy as jnp
from jax import lax
from jax.experimental import pallas as pl
from jax.experimental.pallas import tpu as pltpu
from jax.sharding import PartitionSpec as P

BLOCK = 64
LEVELS = 4
HEAD = 128
NEG = -1e30
AHEAD = 4
MESH = pl.DeviceIdType.MESH
NT = (((1,), (1,)), ((), ()))
TN = (((0,), (0,)), ((), ()))
NN = (((1,), (0,)), ((), ()))


def dot(a, b, dims):
    return lax.dot_general(a, b, dims, preferred_element_type=jnp.float32)


def kernel(
    size, heads, far,
    window_hbm, offsets_hbm, q_hbm, k_hbm, v_hbm, do_hbm,
    att_hbm, gq_hbm, gk_hbm, gv_hbm,
    staged, window, offsets, q_ref, do_ref, tri_low, own, rx1, rx2, rx4, rxf,
    tg1, tg4, ts2, tgf, rg1, rg4, rs2, rgf, hold2, acc,
    send, recv, load, load_small, store,
):
    f32, bf16 = jnp.float32, jnp.bfloat16
    rows = q_hbm.shape[0]
    r = lax.axis_index("ctx")
    odd = lax.rem(r, 2) == 1
    even = jnp.logical_not(odd)
    has_up = r + 2 < size
    scale = HEAD ** -0.5
    mate = r + 1 - 2 * lax.rem(r, 2)

    K_OWN, K_REL, K_PRV, K_G4, K_S2, K_G1, K_FAR = 0, 1, 2, 3, 4, 5, 6
    K_GFAR = K_FAR + len(far)

    def copy(kind, h, src, dst, to):
        return pltpu.make_async_remote_copy(
            src_ref=src, dst_ref=dst, send_sem=send.at[kind, h], recv_sem=recv.at[kind, h],
            device_id={"ctx": to}, device_id_type=MESH,
        )

    def piece(buf, i):
        return buf.at[i // 2, i % 2]

    def own_up(i):
        return copy(K_OWN, i, piece(own, i), piece(rx2, i), r + 2)

    def relay_up(i):
        return copy(K_REL, i, piece(rx2, i), piece(rx4, i), r + 2)

    def prev_own(i):
        return copy(K_PRV, i, piece(own, i), piece(rx1, i), mate)

    def prev_relay(i):
        return copy(K_PRV, i, piece(rx2, i), piece(rx1, i), mate)

    def far_up(n, i):
        return copy(K_FAR + n, i, piece(own, i), piece(rxf.at[n], i), r + far[n])

    def g4_down(i):
        return copy(K_G4, i, piece(tg4, i), piece(rg4, i), r - 2)

    def s2_down(i):
        return copy(K_S2, i, piece(ts2, i), piece(rs2, i), r - 2)

    def g1_mate(i):
        return copy(K_G1, i, piece(tg1, i), piece(rg1, i), mate)

    def gfar_down(n, i):
        return copy(K_GFAR + n, i, piece(tgf.at[n], i), piece(rgf.at[n], i), r - far[n])

    def result(n, h):
        out = (att_hbm, gq_hbm, gk_hbm, gv_hbm)[n]
        return pltpu.make_async_copy(
            staged.at[n, h], out.at[:, h * HEAD:(h + 1) * HEAD], store.at[n, h]
        )

    loads = []
    for h in range(heads):
        cols = slice(h * HEAD, (h + 1) * HEAD)
        loads.append([
            pltpu.make_async_copy(src.at[:, cols], dst, load.at[h, n])
            for n, (src, dst) in enumerate((
                (k_hbm, own.at[h, 0]), (v_hbm, own.at[h, 1]),
                (q_hbm, q_ref.at[h]), (do_hbm, do_ref.at[h]),
            ))
        ])
    small_copies = [
        pltpu.make_async_copy(offsets_hbm, offsets, load_small.at[0]),
        pltpu.make_async_copy(window_hbm, window, load_small.at[1]),
    ]
    for pair in (slice(0, 2), slice(2, 4)):
        for group in loads:
            for c in group[pair]:
                c.start()
    for c in small_copies:
        c.start()

    barrier = pltpu.get_barrier_semaphore()
    pl.semaphore_signal(barrier, inc=1, device_id={"ctx": mate}, device_id_type=MESH)
    count = 1
    for d in (2,) + far:
        for to, ok in ((r + d, r + d < size), (r - d, r >= d)):
            count = count + ok.astype(jnp.int32)

            @pl.when(ok)
            def _(to=to):
                pl.semaphore_signal(barrier, inc=1, device_id={"ctx": to}, device_id_type=MESH)

    for d, buf in ((1, rx1), (2, rx2), (4, rx4)):

        @pl.when(r < d)
        def _(buf=buf):
            buf[...] = jnp.zeros_like(buf)

    for n, d in enumerate(far):

        @pl.when(r < d)
        def _(n=n):
            rxf[n] = jnp.zeros(rxf.shape[1:], bf16)

    pl.semaphore_wait(barrier, count)

    pieces = 2 * heads

    def start_own(i):
        loads[i // 2][i % 2].wait()

        @pl.when(has_up)
        def _():
            own_up(i).start()

        @pl.when(even)
        def _():
            prev_own(i).start()

        for n in range(len(far)):

            @pl.when(r + far[n] < size)
            def _(n=n):
                far_up(n, i).start()

    for i in range(AHEAD):
        start_own(i)
    for group in loads:
        for c in group[2:]:
            c.wait()

    query_i = lax.broadcasted_iota(jnp.int32, (rows, rows), 0)
    key_i = lax.broadcasted_iota(jnp.int32, (rows, rows), 1)
    diff = key_i - query_i
    tri = diff <= 0
    tri_low[0] = jnp.where(tri, 1.0, 0.0).astype(bf16)
    tri_low[1] = jnp.where(diff >= 0, 1.0, 0.0).astype(bf16)
    dists = (2, 4) + far
    wide_log = len(dists) * BLOCK
    lane = lax.broadcasted_iota(jnp.int32, (1, wide_log), 1) // BLOCK
    log_ok = functools.reduce(
        jnp.logical_or, [(lane == j) & (r >= d) for j, d in enumerate(dists)]
    )
    groups = rows // BLOCK
    for c in small_copies:
        c.wait()
    one_row = lax.broadcasted_iota(jnp.int32, (1, HEAD), 1) * 0
    chosen = [
        [
            [
                jnp.where(one_row + (p + d * groups - offsets[p, j]) == place, 1.0, 0.0)
                for place in range(groups)
            ]
            for j, d in enumerate(dists)
        ]
        for p in range(groups)
    ]
    chosen_low = [[[x.astype(bf16) for x in y] for y in z] for z in chosen]

    def block(x, p):
        return x[p * BLOCK:(p + 1) * BLOCK]

    def send_far(i):
        @pl.when(r >= 4)
        def _():
            g4_down(i).start()

        for n in range(len(far)):

            @pl.when(r >= far[n])
            def _(n=n):
                gfar_down(n, i).start()

    def send_near(i):
        @pl.when(r >= 1)
        def _():
            g1_mate(i).start()

    def compute(h):
        q = q_ref[h]
        do = do_ref[h]
        far_bufs = [rx2.at[h], rx4.at[h]] + [rxf.at[n, h] for n in range(len(far))]

        def picked(which):
            arrays = [buf[which] for buf in far_bufs[:len(dists)]]

            def pick(p, j):
                terms = [
                    block(arrays[j], place) * chosen_low[p][j][place] for place in range(groups)
                ]
                return functools.reduce(jnp.add, terms)

            return [
                jnp.concatenate([pick(p, j) for j in range(len(dists))], 0)
                for p in range(groups)
            ]

        arrive(2 * h)
        k_own, k_prev, k_log = own[h, 0], rx1[h, 0], picked(0)

        def against(x, a, b, log):
            near = jnp.where(tri, dot(x, a, NT), dot(x, b, NT))
            return near, jnp.concatenate(
                [dot(block(x, p), log[p], NT) for p in range(groups)], 0
            )

        def weighted(xa, xb, xl, a, b, log):
            return dot(xa, a, NN) + dot(xb, b, NN) + jnp.concatenate(
                [dot(block(xl, p), log[p], NN) for p in range(groups)], 0
            )

        w = window[h]
        limit = jnp.where(r >= 1, rows - w, 2 * rows)
        ok_win = (tri & (diff > -w)) | (diff > limit)
        s_win, s_log = against(q, k_own, k_prev, k_log)
        s_win = jnp.where(ok_win, s_win, NEG)
        s_log = jnp.where(log_ok, s_log, NEG)
        top = jnp.maximum(jnp.max(s_win, 1, keepdims=True), jnp.max(s_log, 1, keepdims=True))
        c = scale * math.log2(math.e)
        w_win = jnp.exp2((s_win - top) * c)
        w_log = jnp.exp2((s_log - top) * c)
        inv = 1.0 / (jnp.sum(w_win, 1, keepdims=True) + jnp.sum(w_log, 1, keepdims=True))
        p_win = w_win * inv
        p_log = w_log * inv
        low = p_win.astype(bf16)
        low_own = low * tri_low[0]
        low_log = p_log.astype(bf16)
        def scattered(parts, j):
            pieces = [block(x, j) for x in parts]
            return jnp.concatenate(
                [
                    functools.reduce(
                        jnp.add, [pieces[p] * chosen[p][j][place] for p in range(groups)]
                    )
                    for place in range(groups)
                ],
                0,
            )

        def keep(which, near, log, x, factor):
            i = 2 * h + which
            parts = [dot(block(log, p), block(x, p), TN) for p in range(groups)]
            for n in range(len(far)):
                tgf[n, h, which] = (scattered(parts, 2 + n) * factor).astype(bf16)
            if len(dists) > 1:
                tg4[h, which] = (scattered(parts, 1) * factor).astype(bf16)
            send_far(i)
            flip = near.T
            flip_own = flip * tri_low[1]
            tg1[h, which] = (dot(flip - flip_own, x, NN) * factor).astype(bf16)
            send_near(i)
            hold2[h, which] = scattered(parts, 0) * factor
            acc[h, which] = dot(flip_own, x, NN) * factor

        keep(1, low, low_log, do, 1.0)
        yield
        arrive(2 * h + 1)
        v_own, v_prev, v_log = own[h, 1], rx1[h, 1], picked(1)
        att = weighted(low_own, low - low_own, low_log, v_own, v_prev, v_log).astype(bf16)
        staged[0, h] = att
        result(0, h).start()
        delta = jnp.sum(att.astype(f32) * do.astype(f32), 1, keepdims=True)
        d_win, d_log = against(do, v_own, v_prev, v_log)
        ds = (p_win * (d_win - delta)).astype(bf16)
        ds_own = ds * tri_low[0]
        ds_log = (p_log * (d_log - delta)).astype(bf16)
        keep(0, ds, ds_log, q, scale)
        gq = weighted(ds_own, ds - ds_own, ds_log, k_own, k_prev, k_log) * scale
        staged[1, h] = gq.astype(bf16)
        result(1, h).start()
        yield

    def combine(i):
        h, w = i // 2, i % 2

        @pl.when((r >= 2) & has_up)
        def _():
            g4_down(i).wait_recv()
            hold2[h, w] = hold2[h, w] + rg4[h, w].astype(f32)

        @pl.when(odd & (r >= 3))
        def _():
            g1_mate(i).wait_recv()
            hold2[h, w] = hold2[h, w] + rg1[h, w].astype(f32)

        @pl.when(r >= 2)
        def _():
            ts2[h, w] = hold2[h, w].astype(bf16)
            s2_down(i).start()

    def relay(i):
        @pl.when(r >= 2)
        def _():
            own_up(i).wait_recv()

        @pl.when((r >= 2) & has_up)
        def _():
            relay_up(i).start()

        @pl.when(odd & (r >= 3))
        def _():
            prev_relay(i).start()

        if i + AHEAD < pieces:
            start_own(i + AHEAD)

    def arrive(i):
        @pl.when(r >= 1)
        def _():
            prev_own(i).wait_recv()

        @pl.when(r >= 4)
        def _():
            relay_up(i).wait_recv()

        for n in range(len(far)):

            @pl.when(r >= far[n])
            def _(n=n):
                far_up(n, i).wait_recv()

    def finish(i):
        h, w = i // 2, i % 2

        @pl.when(even)
        def _():
            g1_mate(i).wait_recv()
            acc[h, w] = acc[h, w] + rg1[h, w].astype(f32)

        for n in range(len(far)):

            @pl.when(r + far[n] < size)
            def _(n=n):
                gfar_down(n, i).wait_recv()
                acc[h, w] = acc[h, w] + rgf[n, h, w].astype(f32)

        @pl.when(has_up)
        def _():
            s2_down(i).wait_recv()
            acc[h, w] = acc[h, w] + rs2[h, w].astype(f32)

        staged[2 + w, h] = acc[h, w].astype(bf16)
        result(2 + w, h).start()

    back = [i for h in range(heads) for i in (2 * h + 1, 2 * h)]
    steps = [compute(h) for h in range(heads)]
    for i in range(AHEAD):
        relay(i)
    for i in range(pieces):
        next(steps[i // 2])
        if i + AHEAD < pieces:
            relay(i + AHEAD)
        if i >= 1:
            combine(back[i - 1])
    combine(back[-1])
    for i in back:
        finish(i)

    for i in range(pieces):

        @pl.when(has_up)
        def _(i=i):
            own_up(i).wait_send()

        @pl.when((r >= 2) & has_up)
        def _(i=i):
            relay_up(i).wait_send()

        @pl.when(even | (r >= 3))
        def _(i=i):
            prev_own(i).wait_send()

        @pl.when(r >= 4)
        def _(i=i):
            g4_down(i).wait_send()

        @pl.when(r >= 2)
        def _(i=i):
            s2_down(i).wait_send()

        @pl.when(r >= 1)
        def _(i=i):
            g1_mate(i).wait_send()

        for n in range(len(far)):

            @pl.when(r + far[n] < size)
            def _(n=n, i=i):
                far_up(n, i).wait_send()

            @pl.when(r >= far[n])
            def _(n=n, i=i):
                gfar_down(n, i).wait_send()

    for n in range(4):
        for h in range(heads):
            result(n, h).wait()


def copy_out(*refs):
    ins, outs, (held, into, back) = refs[:4], refs[4:8], refs[8:]
    first = [pltpu.make_async_copy(ins[n], held.at[n], into.at[n]) for n in range(4)]
    second = [pltpu.make_async_copy(held.at[n], outs[n], back.at[n]) for n in range(4)]
    for c in first:
        c.start()
    for n in range(4):
        first[n].wait()
        second[n].start()
    for c in second:
        c.wait()


def on_device(queries, keys, values, grad_out, window, offsets):
    size = lax.axis_size("ctx")
    rows, feat = queries.shape
    heads = feat // HEAD
    far = tuple(2 ** (j + 1) for j in range(2, LEVELS) if 2 ** (j + 1) < size)
    nf = max(len(far), 1)
    kinds = 6 + 2 * len(far)
    hbm = pl.BlockSpec(memory_space=pltpu.HBM)
    pack = (heads, 2, rows, HEAD)
    small = pltpu.VMEM(pack, jnp.bfloat16)
    wide = pltpu.VMEM(pack, jnp.float32)
    more = pltpu.VMEM((nf,) + (pack if far else (1, 2, 16, HEAD)), jnp.bfloat16)
    out = jax.ShapeDtypeStruct((rows, feat), jnp.bfloat16)
    parts = pl.pallas_call(
        functools.partial(kernel, size, heads, far),
        out_shape=(out,) * 4,
        in_specs=[hbm] * 6,
        out_specs=(hbm,) * 4,
        scratch_shapes=[
            pltpu.VMEM((4, heads, rows, HEAD), jnp.bfloat16),
            pltpu.SMEM(window.shape, jnp.int32),
            pltpu.SMEM(offsets.shape, jnp.int32),
            pltpu.VMEM((heads, rows, HEAD), jnp.bfloat16),
            pltpu.VMEM((heads, rows, HEAD), jnp.bfloat16),
            pltpu.VMEM((2, rows, rows), jnp.bfloat16),
        ]
        + [small] * 4 + [more] + [small] * 3 + [more] + [small] * 3 + [more]
        + [wide] * 2
        + [pltpu.SemaphoreType.DMA((kinds, 2 * heads)), pltpu.SemaphoreType.DMA((kinds, 2 * heads))]
        + [pltpu.SemaphoreType.DMA((heads, 4)), pltpu.SemaphoreType.DMA((2,))]
        + [pltpu.SemaphoreType.DMA((4, heads))],
        compiler_params=pltpu.CompilerParams(
            collective_id=0, has_side_effects=True, vmem_limit_bytes=63 * 2**20
        ),
        cost_estimate=pl.CostEstimate(
            flops=12 * heads * rows * rows * HEAD * (4 + len(far)),
            bytes_accessed=16 * rows * feat,
            transcendentals=heads * rows * rows * (3 + len(far)),
        ),
    )(window, offsets, queries, keys, values, grad_out)
    return pl.pallas_call(
        copy_out,
        out_shape=(out,) * 4,
        in_specs=[hbm] * 4,
        out_specs=(hbm,) * 4,
        scratch_shapes=[
            pltpu.VMEM((4, rows, feat), jnp.bfloat16),
            pltpu.SemaphoreType.DMA((4,)),
            pltpu.SemaphoreType.DMA((4,)),
        ],
        compiler_params=pltpu.CompilerParams(vmem_limit_bytes=63 * 2**20),
        cost_estimate=pl.CostEstimate(
            flops=0, bytes_accessed=16 * rows * feat, transcendentals=0
        ),
    )(*parts)


def solution(mesh):
    cut = P(("dp", "ctx"), None)
    return jax.shard_map(
        on_device,
        mesh=mesh,
        in_specs=(cut, cut, cut, cut, P(), cut),
        out_specs=(cut,) * 4,
        check_vma=False,
    )
```

```python
import functools
import math

import jax
import jax.numpy as jnp
from jax import lax
from jax.experimental import pallas as pl
from jax.experimental.pallas import tpu as pltpu
from jax.sharding import PartitionSpec as P

BLOCK = 64
LEVELS = 4
HEAD = 128
NEG = -1e30
AHEAD = 2
LAG = 2
MESH = pl.DeviceIdType.MESH
NT = (((1,), (1,)), ((), ()))
TN = (((0,), (0,)), ((), ()))
NN = (((1,), (0,)), ((), ()))


def dot(a, b, dims):
    return lax.dot_general(a, b, dims, preferred_element_type=jnp.float32)


def kernel(
    size, heads, far,
    window_hbm, offsets_hbm, q_hbm, k_hbm, v_hbm, do_hbm,
    att_hbm, gq_hbm, gk_hbm, gv_hbm,
    staged, window, offsets, q_ref, do_ref, tri_low, own, rx1, rx2, rx4, rxf,
    tg1, tg4, ts2, tgf, rg1, rg4, rs2, rgf, hold2, acc,
    send, recv, load, load_small, store,
):
    f32, bf16 = jnp.float32, jnp.bfloat16
    rows = q_hbm.shape[0]
    r = lax.axis_index("ctx")
    odd = lax.rem(r, 2) == 1
    even = jnp.logical_not(odd)
    has_up = r + 2 < size
    scale = HEAD ** -0.5
    mate = r + 1 - 2 * lax.rem(r, 2)

    K_OWN, K_REL, K_PRV, K_G4, K_S2, K_G1, K_FAR = 0, 1, 2, 3, 4, 5, 6
    K_GFAR = K_FAR + len(far)

    def copy(kind, h, src, dst, to):
        return pltpu.make_async_remote_copy(
            src_ref=src, dst_ref=dst, send_sem=send.at[kind, h], recv_sem=recv.at[kind, h],
            device_id={"ctx": to}, device_id_type=MESH,
        )

    def piece(buf, i):
        return buf.at[i // 2, i % 2]

    def own_up(i):
        return copy(K_OWN, i, piece(own, i), piece(rx2, i), r + 2)

    def relay_up(i):
        return copy(K_REL, i, piece(rx2, i), piece(rx4, i), r + 2)

    def prev_own(i):
        return copy(K_PRV, i, piece(own, i), piece(rx1, i), mate)

    def prev_relay(i):
        return copy(K_PRV, i, piece(rx2, i), piece(rx1, i), mate)

    def far_up(n, i):
        return copy(K_FAR + n, i, piece(own, i), piece(rxf.at[n], i), r + far[n])

    def g4_down(i):
        return copy(K_G4, i, piece(tg4, i), piece(rg4, i), r - 2)

    def s2_down(i):
        return copy(K_S2, i, piece(ts2, i), piece(rs2, i), r - 2)

    def g1_mate(i):
        return copy(K_G1, i, piece(tg1, i), piece(rg1, i), mate)

    def gfar_down(n, i):
        return copy(K_GFAR + n, i, piece(tgf.at[n], i), piece(rgf.at[n], i), r - far[n])

    def result(n, h):
        out = (att_hbm, gq_hbm, gk_hbm, gv_hbm)[n]
        return pltpu.make_async_copy(
            staged.at[n, h], out.at[:, h * HEAD:(h + 1) * HEAD], store.at[n, h]
        )

    loads = []
    for h in range(heads):
        cols = slice(h * HEAD, (h + 1) * HEAD)
        loads.append([
            pltpu.make_async_copy(src.at[:, cols], dst, load.at[h, n])
            for n, (src, dst) in enumerate((
                (k_hbm, own.at[h, 0]), (v_hbm, own.at[h, 1]),
                (q_hbm, q_ref.at[h]), (do_hbm, do_ref.at[h]),
            ))
        ])
    small_copies = [
        pltpu.make_async_copy(offsets_hbm, offsets, load_small.at[0]),
        pltpu.make_async_copy(window_hbm, window, load_small.at[1]),
    ]
    for pair in (slice(0, 2), slice(2, 4)):
        for group in loads:
            for c in group[pair]:
                c.start()
    for c in small_copies:
        c.start()

    barrier = pltpu.get_barrier_semaphore()
    pl.semaphore_signal(barrier, inc=1, device_id={"ctx": mate}, device_id_type=MESH)
    count = 1
    for d in (2,) + far:
        for to, ok in ((r + d, r + d < size), (r - d, r >= d)):
            count = count + ok.astype(jnp.int32)

            @pl.when(ok)
            def _(to=to):
                pl.semaphore_signal(barrier, inc=1, device_id={"ctx": to}, device_id_type=MESH)

    for d, buf in ((1, rx1), (2, rx2), (4, rx4)):

        @pl.when(r < d)
        def _(buf=buf):
            buf[...] = jnp.zeros_like(buf)

    for n, d in enumerate(far):

        @pl.when(r < d)
        def _(n=n):
            rxf[n] = jnp.zeros(rxf.shape[1:], bf16)

    pl.semaphore_wait(barrier, count)

    pieces = 2 * heads

    def start_own(i):
        loads[i // 2][i % 2].wait()

        @pl.when(has_up)
        def _():
            own_up(i).start()

        @pl.when(even)
        def _():
            prev_own(i).start()

        for n in range(len(far)):

            @pl.when(r + far[n] < size)
            def _(n=n):
                far_up(n, i).start()

    for i in range(AHEAD):
        start_own(i)
    for group in loads:
        for c in group[2:]:
            c.wait()

    query_i = lax.broadcasted_iota(jnp.int32, (rows, rows), 0)
    key_i = lax.broadcasted_iota(jnp.int32, (rows, rows), 1)
    diff = key_i - query_i
    tri = diff <= 0
    tri_low[0] = jnp.where(tri, 1.0, 0.0).astype(bf16)
    tri_low[1] = jnp.where(diff >= 0, 1.0, 0.0).astype(bf16)
    dists = (2, 4) + far
    wide_log = len(dists) * BLOCK
    lane = lax.broadcasted_iota(jnp.int32, (1, wide_log), 1) // BLOCK
    log_ok = functools.reduce(
        jnp.logical_or, [(lane == j) & (r >= d) for j, d in enumerate(dists)]
    )
    groups = rows // BLOCK
    for c in small_copies:
        c.wait()
    one_row = lax.broadcasted_iota(jnp.int32, (1, HEAD), 1) * 0
    chosen = [
        [
            [
                jnp.where(one_row + (p + d * groups - offsets[p, j]) == place, 1.0, 0.0)
                for place in range(groups)
            ]
            for j, d in enumerate(dists)
        ]
        for p in range(groups)
    ]
    chosen_low = [[[x.astype(bf16) for x in y] for y in z] for z in chosen]

    def block(x, p):
        return x[p * BLOCK:(p + 1) * BLOCK]

    def send_far(i):
        @pl.when(r >= 4)
        def _():
            g4_down(i).start()

        for n in range(len(far)):

            @pl.when(r >= far[n])
            def _(n=n):
                gfar_down(n, i).start()

    def send_near(i):
        @pl.when(r >= 1)
        def _():
            g1_mate(i).start()

    def compute(h):
        q = q_ref[h]
        do = do_ref[h]
        far_bufs = [rx2.at[h], rx4.at[h]] + [rxf.at[n, h] for n in range(len(far))]

        def picked(which):
            arrays = [buf[which] for buf in far_bufs[:len(dists)]]

            def pick(p, j):
                terms = [
                    block(arrays[j], place) * chosen_low[p][j][place] for place in range(groups)
                ]
                return functools.reduce(jnp.add, terms)

            return [
                jnp.concatenate([pick(p, j) for j in range(len(dists))], 0)
                for p in range(groups)
            ]

        arrive(2 * h)
        k_own, k_prev, k_log = own[h, 0], rx1[h, 0], picked(0)

        def against(x, a, b, log):
            near = jnp.where(tri, dot(x, a, NT), dot(x, b, NT))
            return near, jnp.concatenate(
                [dot(block(x, p), log[p], NT) for p in range(groups)], 0
            )

        def weighted(xa, xb, xl, a, b, log):
            return dot(xa, a, NN) + dot(xb, b, NN) + jnp.concatenate(
                [dot(block(xl, p), log[p], NN) for p in range(groups)], 0
            )

        w = window[h]
        limit = jnp.where(r >= 1, rows - w, 2 * rows)
        ok_win = (tri & (diff > -w)) | (diff > limit)
        s_win, s_log = against(q, k_own, k_prev, k_log)
        s_win = jnp.where(ok_win, s_win, NEG)
        s_log = jnp.where(log_ok, s_log, NEG)
        top = jnp.maximum(jnp.max(s_win, 1, keepdims=True), jnp.max(s_log, 1, keepdims=True))
        c = scale * math.log2(math.e)
        w_win = jnp.exp2((s_win - top) * c)
        w_log = jnp.exp2((s_log - top) * c)
        inv = 1.0 / (jnp.sum(w_win, 1, keepdims=True) + jnp.sum(w_log, 1, keepdims=True))
        p_win = w_win * inv
        p_log = w_log * inv
        low = p_win.astype(bf16)
        low_own = low * tri_low[0]
        low_log = p_log.astype(bf16)
        def scattered(parts, j):
            pieces = [block(x, j) for x in parts]
            return jnp.concatenate(
                [
                    functools.reduce(
                        jnp.add, [pieces[p] * chosen[p][j][place] for p in range(groups)]
                    )
                    for place in range(groups)
                ],
                0,
            )

        def keep(which, near, log, x, factor):
            i = 2 * h + which
            parts = [dot(block(log, p), block(x, p), TN) for p in range(groups)]
            for n in range(len(far)):
                tgf[n, h, which] = (scattered(parts, 2 + n) * factor).astype(bf16)
            if len(dists) > 1:
                tg4[h, which] = (scattered(parts, 1) * factor).astype(bf16)
            send_far(i)
            flip = near.T
            flip_own = flip * tri_low[1]
            tg1[h, which] = (dot(flip - flip_own, x, NN) * factor).astype(bf16)
            send_near(i)
            hold2[h, which] = scattered(parts, 0) * factor
            acc[h, which] = dot(flip_own, x, NN) * factor

        keep(1, low, low_log, do, 1.0)
        yield
        arrive(2 * h + 1)
        v_own, v_prev, v_log = own[h, 1], rx1[h, 1], picked(1)
        att = weighted(low_own, low - low_own, low_log, v_own, v_prev, v_log).astype(bf16)
        staged[0, h] = att
        result(0, h).start()
        delta = jnp.sum(att.astype(f32) * do.astype(f32), 1, keepdims=True)
        d_win, d_log = against(do, v_own, v_prev, v_log)
        ds = (p_win * (d_win - delta)).astype(bf16)
        ds_own = ds * tri_low[0]
        ds_log = (p_log * (d_log - delta)).astype(bf16)
        keep(0, ds, ds_log, q, scale)
        gq = weighted(ds_own, ds - ds_own, ds_log, k_own, k_prev, k_log) * scale
        staged[1, h] = gq.astype(bf16)
        result(1, h).start()
        yield

    def combine(i):
        h, w = i // 2, i % 2

        @pl.when((r >= 2) & has_up)
        def _():
            g4_down(i).wait_recv()
            hold2[h, w] = hold2[h, w] + rg4[h, w].astype(f32)

        @pl.when(odd & (r >= 3))
        def _():
            g1_mate(i).wait_recv()
            hold2[h, w] = hold2[h, w] + rg1[h, w].astype(f32)

        @pl.when(r >= 2)
        def _():
            ts2[h, w] = hold2[h, w].astype(bf16)
            s2_down(i).start()

    def relay(i):
        @pl.when(r >= 2)
        def _():
            own_up(i).wait_recv()

        @pl.when((r >= 2) & has_up)
        def _():
            relay_up(i).start()

        @pl.when(odd & (r >= 3))
        def _():
            prev_relay(i).start()

        if i + AHEAD < pieces:
            start_own(i + AHEAD)

    def arrive(i):
        @pl.when(r >= 1)
        def _():
            prev_own(i).wait_recv()

        @pl.when(r >= 4)
        def _():
            relay_up(i).wait_recv()

        for n in range(len(far)):

            @pl.when(r >= far[n])
            def _(n=n):
                far_up(n, i).wait_recv()

    def finish(i):
        h, w = i // 2, i % 2

        @pl.when(even)
        def _():
            g1_mate(i).wait_recv()
            acc[h, w] = acc[h, w] + rg1[h, w].astype(f32)

        for n in range(len(far)):

            @pl.when(r + far[n] < size)
            def _(n=n):
                gfar_down(n, i).wait_recv()
                acc[h, w] = acc[h, w] + rgf[n, h, w].astype(f32)

        @pl.when(has_up)
        def _():
            s2_down(i).wait_recv()
            acc[h, w] = acc[h, w] + rs2[h, w].astype(f32)

        staged[2 + w, h] = acc[h, w].astype(bf16)
        result(2 + w, h).start()

    back = [i for h in range(heads) for i in (2 * h + 1, 2 * h)]
    steps = [compute(h) for h in range(heads)]
    for i in range(AHEAD):
        relay(i)
    for i in range(pieces):
        next(steps[i // 2])
        if i + AHEAD < pieces:
            relay(i + AHEAD)
        if i >= LAG:
            combine(back[i - LAG])
    for i in back[-LAG:]:
        combine(i)
    for i in back:
        finish(i)

    for i in range(pieces):

        @pl.when(has_up)
        def _(i=i):
            own_up(i).wait_send()

        @pl.when((r >= 2) & has_up)
        def _(i=i):
            relay_up(i).wait_send()

        @pl.when(even | (r >= 3))
        def _(i=i):
            prev_own(i).wait_send()

        @pl.when(r >= 4)
        def _(i=i):
            g4_down(i).wait_send()

        @pl.when(r >= 2)
        def _(i=i):
            s2_down(i).wait_send()

        @pl.when(r >= 1)
        def _(i=i):
            g1_mate(i).wait_send()

        for n in range(len(far)):

            @pl.when(r + far[n] < size)
            def _(n=n, i=i):
                far_up(n, i).wait_send()

            @pl.when(r >= far[n])
            def _(n=n, i=i):
                gfar_down(n, i).wait_send()

    for n in range(4):
        for h in range(heads):
            result(n, h).wait()


def copy_out(*refs):
    ins, outs, (held, into, back) = refs[:4], refs[4:8], refs[8:]
    first = [pltpu.make_async_copy(ins[n], held.at[n], into.at[n]) for n in range(4)]
    second = [pltpu.make_async_copy(held.at[n], outs[n], back.at[n]) for n in range(4)]
    for c in first:
        c.start()
    for n in range(4):
        first[n].wait()
        second[n].start()
    for c in second:
        c.wait()


def on_device(queries, keys, values, grad_out, window, offsets):
    size = lax.axis_size("ctx")
    rows, feat = queries.shape
    heads = feat // HEAD
    far = tuple(2 ** (j + 1) for j in range(2, LEVELS) if 2 ** (j + 1) < size)
    nf = max(len(far), 1)
    kinds = 6 + 2 * len(far)
    hbm = pl.BlockSpec(memory_space=pltpu.HBM)
    pack = (heads, 2, rows, HEAD)
    small = pltpu.VMEM(pack, jnp.bfloat16)
    wide = pltpu.VMEM(pack, jnp.float32)
    more = pltpu.VMEM((nf,) + (pack if far else (1, 2, 16, HEAD)), jnp.bfloat16)
    out = jax.ShapeDtypeStruct((rows, feat), jnp.bfloat16)
    parts = pl.pallas_call(
        functools.partial(kernel, size, heads, far),
        out_shape=(out,) * 4,
        in_specs=[hbm] * 6,
        out_specs=(hbm,) * 4,
        scratch_shapes=[
            pltpu.VMEM((4, heads, rows, HEAD), jnp.bfloat16),
            pltpu.SMEM(window.shape, jnp.int32),
            pltpu.SMEM(offsets.shape, jnp.int32),
            pltpu.VMEM((heads, rows, HEAD), jnp.bfloat16),
            pltpu.VMEM((heads, rows, HEAD), jnp.bfloat16),
            pltpu.VMEM((2, rows, rows), jnp.bfloat16),
        ]
        + [small] * 4 + [more] + [small] * 3 + [more] + [small] * 3 + [more]
        + [wide] * 2
        + [pltpu.SemaphoreType.DMA((kinds, 2 * heads)), pltpu.SemaphoreType.DMA((kinds, 2 * heads))]
        + [pltpu.SemaphoreType.DMA((heads, 4)), pltpu.SemaphoreType.DMA((2,))]
        + [pltpu.SemaphoreType.DMA((4, heads))],
        compiler_params=pltpu.CompilerParams(
            collective_id=0, has_side_effects=True, vmem_limit_bytes=63 * 2**20
        ),
        cost_estimate=pl.CostEstimate(
            flops=12 * heads * rows * rows * HEAD * (4 + len(far)),
            bytes_accessed=16 * rows * feat,
            transcendentals=heads * rows * rows * (3 + len(far)),
        ),
    )(window, offsets, queries, keys, values, grad_out)
    return pl.pallas_call(
        copy_out,
        out_shape=(out,) * 4,
        in_specs=[hbm] * 4,
        out_specs=(hbm,) * 4,
        scratch_shapes=[
            pltpu.VMEM((4, rows, feat), jnp.bfloat16),
            pltpu.SemaphoreType.DMA((4,)),
            pltpu.SemaphoreType.DMA((4,)),
        ],
        compiler_params=pltpu.CompilerParams(vmem_limit_bytes=63 * 2**20),
        cost_estimate=pl.CostEstimate(
            flops=0, bytes_accessed=16 * rows * feat, transcendentals=0
        ),
    )(*parts)


def solution(mesh):
    cut = P(("dp", "ctx"), None)
    return jax.shard_map(
        on_device,
        mesh=mesh,
        in_specs=(cut, cut, cut, cut, P(), cut),
        out_specs=(cut,) * 4,
        check_vma=False,
    )
```

```python
import functools
import math

import jax
import jax.numpy as jnp
from jax import lax
from jax.experimental import pallas as pl
from jax.experimental.pallas import tpu as pltpu
from jax.sharding import PartitionSpec as P

BLOCK = 64
LEVELS = 4
HEAD = 128
NEG = -1e30
AHEAD = 2
LAG = 2
MESH = pl.DeviceIdType.MESH
NT = (((1,), (1,)), ((), ()))
TN = (((0,), (0,)), ((), ()))
NN = (((1,), (0,)), ((), ()))


def dot(a, b, dims):
    return lax.dot_general(a, b, dims, preferred_element_type=jnp.float32)


def kernel(
    size, heads, far,
    window_hbm, offsets_hbm, q_hbm, k_hbm, v_hbm, do_hbm,
    att_hbm, gq_hbm, gk_hbm, gv_hbm,
    staged, window, offsets, q_ref, do_ref, tri_low, own, rx1, rx2, rx4, rxf,
    tg1, tg4, ts2, tgf, rg1, rg4, rs2, rgf, hold2, acc,
    send, recv, load, load_small, store,
):
    f32, bf16 = jnp.float32, jnp.bfloat16
    rows = q_hbm.shape[0]
    r = lax.axis_index("ctx")
    odd = lax.rem(r, 2) == 1
    even = jnp.logical_not(odd)
    has_up = r + 2 < size
    scale = HEAD ** -0.5
    mate = r + 1 - 2 * lax.rem(r, 2)

    K_OWN, K_REL, K_PRV, K_G4, K_S2, K_G1, K_FAR = 0, 1, 2, 3, 4, 5, 6
    K_GFAR = K_FAR + len(far)

    def copy(kind, h, src, dst, to):
        return pltpu.make_async_remote_copy(
            src_ref=src, dst_ref=dst, send_sem=send.at[kind, h], recv_sem=recv.at[kind, h],
            device_id={"ctx": to}, device_id_type=MESH,
        )

    def piece(buf, i):
        return buf.at[i // 2, i % 2]

    def own_up(i):
        return copy(K_OWN, i, piece(own, i), piece(rx2, i), r + 2)

    def relay_up(i):
        return copy(K_REL, i, piece(rx2, i), piece(rx4, i), r + 2)

    def prev_own(i):
        return copy(K_PRV, i, piece(own, i), piece(rx1, i), mate)

    def prev_relay(i):
        return copy(K_PRV, i, piece(rx2, i), piece(rx1, i), mate)

    def far_up(n, i):
        return copy(K_FAR + n, i, piece(own, i), piece(rxf.at[n], i), r + far[n])

    def g4_down(i):
        return copy(K_G4, i, piece(tg4, i), piece(rg4, i), r - 2)

    def s2_down(i):
        return copy(K_S2, i, piece(ts2, i), piece(rs2, i), r - 2)

    def g1_mate(i):
        return copy(K_G1, i, piece(tg1, i), piece(rg1, i), mate)

    def gfar_down(n, i):
        return copy(K_GFAR + n, i, piece(tgf.at[n], i), piece(rgf.at[n], i), r - far[n])

    def result(n, h):
        out = (att_hbm, gq_hbm, gk_hbm, gv_hbm)[n]
        return pltpu.make_async_copy(
            staged.at[n, h], out.at[:, h * HEAD:(h + 1) * HEAD], store.at[n, h]
        )

    loads = []
    for h in range(heads):
        cols = slice(h * HEAD, (h + 1) * HEAD)
        loads.append([
            pltpu.make_async_copy(src.at[:, cols], dst, load.at[h, n])
            for n, (src, dst) in enumerate((
                (k_hbm, own.at[h, 0]), (v_hbm, own.at[h, 1]),
                (q_hbm, q_ref.at[h]), (do_hbm, do_ref.at[h]),
            ))
        ])
    small_copies = [
        pltpu.make_async_copy(offsets_hbm, offsets, load_small.at[0]),
        pltpu.make_async_copy(window_hbm, window, load_small.at[1]),
    ]
    for pair in (slice(0, 2), slice(2, 4)):
        for group in loads:
            for c in group[pair]:
                c.start()
    for c in small_copies:
        c.start()

    barrier = pltpu.get_barrier_semaphore()
    pl.semaphore_signal(barrier, inc=1, device_id={"ctx": mate}, device_id_type=MESH)
    count = 1
    for d in (2,) + far:
        for to, ok in ((r + d, r + d < size), (r - d, r >= d)):
            count = count + ok.astype(jnp.int32)

            @pl.when(ok)
            def _(to=to):
                pl.semaphore_signal(barrier, inc=1, device_id={"ctx": to}, device_id_type=MESH)

    for d, buf in ((1, rx1), (2, rx2), (4, rx4)):

        @pl.when(r < d)
        def _(buf=buf):
            buf[...] = jnp.zeros_like(buf)

    for n, d in enumerate(far):

        @pl.when(r < d)
        def _(n=n):
            rxf[n] = jnp.zeros(rxf.shape[1:], bf16)

    pl.semaphore_wait(barrier, count)

    pieces = 2 * heads

    def start_own(i):
        loads[i // 2][i % 2].wait()

        @pl.when(even)
        def _():
            prev_own(i).start()

        @pl.when(has_up)
        def _():
            own_up(i).start()

        for n in range(len(far)):

            @pl.when(r + far[n] < size)
            def _(n=n):
                far_up(n, i).start()

    for i in range(AHEAD):
        start_own(i)
    for group in loads:
        for c in group[2:]:
            c.wait()

    query_i = lax.broadcasted_iota(jnp.int32, (rows, rows), 0)
    key_i = lax.broadcasted_iota(jnp.int32, (rows, rows), 1)
    diff = key_i - query_i
    tri = diff <= 0
    tri_low[0] = jnp.where(tri, 1.0, 0.0).astype(bf16)
    tri_low[1] = jnp.where(diff >= 0, 1.0, 0.0).astype(bf16)
    dists = (2, 4) + far
    wide_log = len(dists) * BLOCK
    lane = lax.broadcasted_iota(jnp.int32, (1, wide_log), 1) // BLOCK
    log_ok = functools.reduce(
        jnp.logical_or, [(lane == j) & (r >= d) for j, d in enumerate(dists)]
    )
    groups = rows // BLOCK
    for c in small_copies:
        c.wait()
    one_row = lax.broadcasted_iota(jnp.int32, (1, HEAD), 1) * 0
    chosen = [
        [
            [
                jnp.where(one_row + (p + d * groups - offsets[p, j]) == place, 1.0, 0.0)
                for place in range(groups)
            ]
            for j, d in enumerate(dists)
        ]
        for p in range(groups)
    ]
    chosen_low = [[[x.astype(bf16) for x in y] for y in z] for z in chosen]

    def block(x, p):
        return x[p * BLOCK:(p + 1) * BLOCK]

    def send_far(i):
        @pl.when(r >= 4)
        def _():
            g4_down(i).start()

        for n in range(len(far)):

            @pl.when(r >= far[n])
            def _(n=n):
                gfar_down(n, i).start()

    def send_near(i):
        @pl.when(r >= 1)
        def _():
            g1_mate(i).start()

    def compute(h):
        q = q_ref[h]
        do = do_ref[h]
        far_bufs = [rx2.at[h], rx4.at[h]] + [rxf.at[n, h] for n in range(len(far))]

        def picked(which):
            arrays = [buf[which] for buf in far_bufs[:len(dists)]]

            def pick(p, j):
                terms = [
                    block(arrays[j], place) * chosen_low[p][j][place] for place in range(groups)
                ]
                return functools.reduce(jnp.add, terms)

            return [
                jnp.concatenate([pick(p, j) for j in range(len(dists))], 0)
                for p in range(groups)
            ]

        arrive(2 * h)
        k_own, k_prev, k_log = own[h, 0], rx1[h, 0], picked(0)

        def against(x, a, b, log):
            near = jnp.where(tri, dot(x, a, NT), dot(x, b, NT))
            return near, jnp.concatenate(
                [dot(block(x, p), log[p], NT) for p in range(groups)], 0
            )

        def weighted(xa, xb, xl, a, b, log):
            return dot(xa, a, NN) + dot(xb, b, NN) + jnp.concatenate(
                [dot(block(xl, p), log[p], NN) for p in range(groups)], 0
            )

        w = window[h]
        limit = jnp.where(r >= 1, rows - w, 2 * rows)
        ok_win = (tri & (diff > -w)) | (diff > limit)
        s_win, s_log = against(q, k_own, k_prev, k_log)
        s_win = jnp.where(ok_win, s_win, NEG)
        s_log = jnp.where(log_ok, s_log, NEG)
        top = jnp.maximum(jnp.max(s_win, 1, keepdims=True), jnp.max(s_log, 1, keepdims=True))
        c = scale * math.log2(math.e)
        w_win = jnp.exp2((s_win - top) * c)
        w_log = jnp.exp2((s_log - top) * c)
        inv = 1.0 / (jnp.sum(w_win, 1, keepdims=True) + jnp.sum(w_log, 1, keepdims=True))
        p_win = w_win * inv
        p_log = w_log * inv
        low = p_win.astype(bf16)
        low_own = low * tri_low[0]
        low_log = p_log.astype(bf16)
        def scattered(parts, j):
            pieces = [block(x, j) for x in parts]
            return jnp.concatenate(
                [
                    functools.reduce(
                        jnp.add, [pieces[p] * chosen[p][j][place] for p in range(groups)]
                    )
                    for place in range(groups)
                ],
                0,
            )

        def keep(which, near, log, x, factor):
            i = 2 * h + which
            parts = [dot(block(log, p), block(x, p), TN) for p in range(groups)]
            flip = near.T
            flip_own = flip * tri_low[1]
            tg1[h, which] = (dot(flip - flip_own, x, NN) * factor).astype(bf16)
            send_near(i)
            for n in range(len(far)):
                tgf[n, h, which] = (scattered(parts, 2 + n) * factor).astype(bf16)
            if len(dists) > 1:
                tg4[h, which] = (scattered(parts, 1) * factor).astype(bf16)
            send_far(i)
            hold2[h, which] = scattered(parts, 0) * factor
            acc[h, which] = dot(flip_own, x, NN) * factor

        keep(1, low, low_log, do, 1.0)
        yield
        arrive(2 * h + 1)
        v_own, v_prev, v_log = own[h, 1], rx1[h, 1], picked(1)
        att = weighted(low_own, low - low_own, low_log, v_own, v_prev, v_log).astype(bf16)
        staged[0, h] = att
        result(0, h).start()
        delta = jnp.sum(att.astype(f32) * do.astype(f32), 1, keepdims=True)
        d_win, d_log = against(do, v_own, v_prev, v_log)
        ds = (p_win * (d_win - delta)).astype(bf16)
        ds_own = ds * tri_low[0]
        ds_log = (p_log * (d_log - delta)).astype(bf16)
        keep(0, ds, ds_log, q, scale)
        gq = weighted(ds_own, ds - ds_own, ds_log, k_own, k_prev, k_log) * scale
        staged[1, h] = gq.astype(bf16)
        result(1, h).start()
        yield

    def combine(i):
        h, w = i // 2, i % 2

        @pl.when((r >= 2) & has_up)
        def _():
            g4_down(i).wait_recv()
            hold2[h, w] = hold2[h, w] + rg4[h, w].astype(f32)

        @pl.when(odd & (r >= 3))
        def _():
            g1_mate(i).wait_recv()
            hold2[h, w] = hold2[h, w] + rg1[h, w].astype(f32)

        @pl.when(r >= 2)
        def _():
            ts2[h, w] = hold2[h, w].astype(bf16)
            s2_down(i).start()

    def relay(i):
        @pl.when(r >= 2)
        def _():
            own_up(i).wait_recv()

        @pl.when(odd & (r >= 3))
        def _():
            prev_relay(i).start()

        @pl.when((r >= 2) & has_up)
        def _():
            relay_up(i).start()

        if i + AHEAD < pieces:
            start_own(i + AHEAD)

    def arrive(i):
        @pl.when(r >= 1)
        def _():
            prev_own(i).wait_recv()

        @pl.when(r >= 4)
        def _():
            relay_up(i).wait_recv()

        for n in range(len(far)):

            @pl.when(r >= far[n])
            def _(n=n):
                far_up(n, i).wait_recv()

    def finish(i):
        h, w = i // 2, i % 2

        @pl.when(even)
        def _():
            g1_mate(i).wait_recv()
            acc[h, w] = acc[h, w] + rg1[h, w].astype(f32)

        for n in range(len(far)):

            @pl.when(r + far[n] < size)
            def _(n=n):
                gfar_down(n, i).wait_recv()
                acc[h, w] = acc[h, w] + rgf[n, h, w].astype(f32)

        @pl.when(has_up)
        def _():
            s2_down(i).wait_recv()
            acc[h, w] = acc[h, w] + rs2[h, w].astype(f32)

        staged[2 + w, h] = acc[h, w].astype(bf16)
        result(2 + w, h).start()

    back = [i for h in range(heads) for i in (2 * h + 1, 2 * h)]
    steps = [compute(h) for h in range(heads)]
    for i in range(AHEAD):
        relay(i)
    for i in range(pieces):
        next(steps[i // 2])
        if i + AHEAD < pieces:
            relay(i + AHEAD)
        if i >= LAG:
            combine(back[i - LAG])
    for i in back[-LAG:]:
        combine(i)
    for i in back:
        finish(i)

    for i in range(pieces):

        @pl.when(has_up)
        def _(i=i):
            own_up(i).wait_send()

        @pl.when((r >= 2) & has_up)
        def _(i=i):
            relay_up(i).wait_send()

        @pl.when(even | (r >= 3))
        def _(i=i):
            prev_own(i).wait_send()

        @pl.when(r >= 4)
        def _(i=i):
            g4_down(i).wait_send()

        @pl.when(r >= 2)
        def _(i=i):
            s2_down(i).wait_send()

        @pl.when(r >= 1)
        def _(i=i):
            g1_mate(i).wait_send()

        for n in range(len(far)):

            @pl.when(r + far[n] < size)
            def _(n=n, i=i):
                far_up(n, i).wait_send()

            @pl.when(r >= far[n])
            def _(n=n, i=i):
                gfar_down(n, i).wait_send()

    for n in range(4):
        for h in range(heads):
            result(n, h).wait()


def copy_out(*refs):
    ins, outs, (held, into, back) = refs[:4], refs[4:8], refs[8:]
    first = [pltpu.make_async_copy(ins[n], held.at[n], into.at[n]) for n in range(4)]
    second = [pltpu.make_async_copy(held.at[n], outs[n], back.at[n]) for n in range(4)]
    for c in first:
        c.start()
    for n in range(4):
        first[n].wait()
        second[n].start()
    for c in second:
        c.wait()


def on_device(queries, keys, values, grad_out, window, offsets):
    size = lax.axis_size("ctx")
    rows, feat = queries.shape
    heads = feat // HEAD
    far = tuple(2 ** (j + 1) for j in range(2, LEVELS) if 2 ** (j + 1) < size)
    nf = max(len(far), 1)
    kinds = 6 + 2 * len(far)
    hbm = pl.BlockSpec(memory_space=pltpu.HBM)
    pack = (heads, 2, rows, HEAD)
    small = pltpu.VMEM(pack, jnp.bfloat16)
    wide = pltpu.VMEM(pack, jnp.float32)
    more = pltpu.VMEM((nf,) + (pack if far else (1, 2, 16, HEAD)), jnp.bfloat16)
    out = jax.ShapeDtypeStruct((rows, feat), jnp.bfloat16)
    parts = pl.pallas_call(
        functools.partial(kernel, size, heads, far),
        out_shape=(out,) * 4,
        in_specs=[hbm] * 6,
        out_specs=(hbm,) * 4,
        scratch_shapes=[
            pltpu.VMEM((4, heads, rows, HEAD), jnp.bfloat16),
            pltpu.SMEM(window.shape, jnp.int32),
            pltpu.SMEM(offsets.shape, jnp.int32),
            pltpu.VMEM((heads, rows, HEAD), jnp.bfloat16),
            pltpu.VMEM((heads, rows, HEAD), jnp.bfloat16),
            pltpu.VMEM((2, rows, rows), jnp.bfloat16),
        ]
        + [small] * 4 + [more] + [small] * 3 + [more] + [small] * 3 + [more]
        + [wide] * 2
        + [pltpu.SemaphoreType.DMA((kinds, 2 * heads)), pltpu.SemaphoreType.DMA((kinds, 2 * heads))]
        + [pltpu.SemaphoreType.DMA((heads, 4)), pltpu.SemaphoreType.DMA((2,))]
        + [pltpu.SemaphoreType.DMA((4, heads))],
        compiler_params=pltpu.CompilerParams(
            collective_id=0, has_side_effects=True, vmem_limit_bytes=63 * 2**20
        ),
        cost_estimate=pl.CostEstimate(
            flops=12 * heads * rows * rows * HEAD * (4 + len(far)),
            bytes_accessed=16 * rows * feat,
            transcendentals=heads * rows * rows * (3 + len(far)),
        ),
    )(window, offsets, queries, keys, values, grad_out)
    return pl.pallas_call(
        copy_out,
        out_shape=(out,) * 4,
        in_specs=[hbm] * 4,
        out_specs=(hbm,) * 4,
        scratch_shapes=[
            pltpu.VMEM((4, rows, feat), jnp.bfloat16),
            pltpu.SemaphoreType.DMA((4,)),
            pltpu.SemaphoreType.DMA((4,)),
        ],
        compiler_params=pltpu.CompilerParams(vmem_limit_bytes=63 * 2**20),
        cost_estimate=pl.CostEstimate(
            flops=0, bytes_accessed=16 * rows * feat, transcendentals=0
        ),
    )(*parts)


def solution(mesh):
    cut = P(("dp", "ctx"), None)
    return jax.shard_map(
        on_device,
        mesh=mesh,
        in_specs=(cut, cut, cut, cut, P(), cut),
        out_specs=(cut,) * 4,
        check_vma=False,
    )
```

```python
import functools
import math

import jax
import jax.numpy as jnp
from jax import lax
from jax.experimental import pallas as pl
from jax.experimental.pallas import tpu as pltpu
from jax.sharding import PartitionSpec as P

BLOCK = 64
LEVELS = 4
HEAD = 128
NEG = -1e30
AHEAD = 2
LAG = 2
MESH = pl.DeviceIdType.MESH
NT = (((1,), (1,)), ((), ()))
TN = (((0,), (0,)), ((), ()))
NN = (((1,), (0,)), ((), ()))


def dot(a, b, dims):
    return lax.dot_general(a, b, dims, preferred_element_type=jnp.float32)


def kernel(
    size, heads, far,
    window_hbm, offsets_hbm, q_hbm, k_hbm, v_hbm, do_hbm,
    att_hbm, gq_hbm, gk_hbm, gv_hbm,
    staged, window, offsets, q_ref, do_ref, tri_low, own, rx1, rx2, rx4, rxf,
    tg1, tg4, ts2, tgf, rg1, rg4, rs2, rgf, hold2, acc,
    send, recv, load, load_small, store,
):
    f32, bf16 = jnp.float32, jnp.bfloat16
    rows = q_hbm.shape[0]
    r = lax.axis_index("ctx")
    odd = lax.rem(r, 2) == 1
    even = jnp.logical_not(odd)
    has_up = r + 2 < size
    scale = HEAD ** -0.5
    mate = r + 1 - 2 * lax.rem(r, 2)

    K_OWN, K_REL, K_PRV, K_G4, K_S2, K_G1, K_FAR = 0, 1, 2, 3, 4, 5, 6
    K_GFAR = K_FAR + len(far)

    def copy(kind, h, src, dst, to):
        return pltpu.make_async_remote_copy(
            src_ref=src, dst_ref=dst, send_sem=send.at[kind, h], recv_sem=recv.at[kind, h],
            device_id={"ctx": to}, device_id_type=MESH,
        )

    def piece(buf, i):
        return buf.at[i // 2, i % 2]

    def own_up(i):
        return copy(K_OWN, i, piece(own, i), piece(rx2, i), r + 2)

    def relay_up(i):
        return copy(K_REL, i, piece(rx2, i), piece(rx4, i), r + 2)

    def prev_own(i):
        return copy(K_PRV, i, piece(own, i), piece(rx1, i), mate)

    def prev_relay(i):
        return copy(K_PRV, i, piece(rx2, i), piece(rx1, i), mate)

    def far_up(n, i):
        return copy(K_FAR + n, i, piece(own, i), piece(rxf.at[n], i), r + far[n])

    def g4_down(i):
        return copy(K_G4, i, piece(tg4, i), piece(rg4, i), r - 2)

    def s2_down(i):
        return copy(K_S2, i, piece(ts2, i), piece(rs2, i), r - 2)

    def g1_mate(i):
        return copy(K_G1, i, piece(tg1, i), piece(rg1, i), mate)

    def gfar_down(n, i):
        return copy(K_GFAR + n, i, piece(tgf.at[n], i), piece(rgf.at[n], i), r - far[n])

    def result(n, h):
        out = (att_hbm, gq_hbm, gk_hbm, gv_hbm)[n]
        return pltpu.make_async_copy(
            staged.at[n, h], out.at[:, h * HEAD:(h + 1) * HEAD], store.at[n, h]
        )

    loads = []
    for h in range(heads):
        cols = slice(h * HEAD, (h + 1) * HEAD)
        loads.append([
            pltpu.make_async_copy(src.at[:, cols], dst, load.at[h, n])
            for n, (src, dst) in enumerate((
                (k_hbm, own.at[h, 0]), (v_hbm, own.at[h, 1]),
                (q_hbm, q_ref.at[h]), (do_hbm, do_ref.at[h]),
            ))
        ])
    small_copies = [
        pltpu.make_async_copy(offsets_hbm, offsets, load_small.at[0]),
        pltpu.make_async_copy(window_hbm, window, load_small.at[1]),
    ]
    for pair in (slice(0, 2), slice(2, 4)):
        for group in loads:
            for c in group[pair]:
                c.start()
    for c in small_copies:
        c.start()

    barrier = pltpu.get_barrier_semaphore()
    pl.semaphore_signal(barrier, inc=1, device_id={"ctx": mate}, device_id_type=MESH)
    count = 1
    for d in (2,) + far:
        for to, ok in ((r + d, r + d < size), (r - d, r >= d)):
            count = count + ok.astype(jnp.int32)

            @pl.when(ok)
            def _(to=to):
                pl.semaphore_signal(barrier, inc=1, device_id={"ctx": to}, device_id_type=MESH)

    for d, buf in ((1, rx1), (2, rx2), (4, rx4)):

        @pl.when(r < d)
        def _(buf=buf):
            buf[...] = jnp.zeros_like(buf)

    for n, d in enumerate(far):

        @pl.when(r < d)
        def _(n=n):
            rxf[n] = jnp.zeros(rxf.shape[1:], bf16)

    pl.semaphore_wait(barrier, count)

    pieces = 2 * heads

    def start_own(i):
        loads[i // 2][i % 2].wait()

        @pl.when(even)
        def _():
            prev_own(i).start()

        @pl.when(has_up)
        def _():
            own_up(i).start()

        for n in range(len(far)):

            @pl.when(r + far[n] < size)
            def _(n=n):
                far_up(n, i).start()

    for i in range(AHEAD):
        start_own(i)
    for group in loads:
        for c in group[2:]:
            c.wait()

    query_i = lax.broadcasted_iota(jnp.int32, (rows, rows), 0)
    key_i = lax.broadcasted_iota(jnp.int32, (rows, rows), 1)
    diff = key_i - query_i
    tri = diff <= 0
    tri_low[0] = jnp.where(tri, 1.0, 0.0).astype(bf16)
    tri_low[1] = jnp.where(diff >= 0, 1.0, 0.0).astype(bf16)
    dists = (2, 4) + far
    wide_log = len(dists) * BLOCK
    lane = lax.broadcasted_iota(jnp.int32, (1, wide_log), 1) // BLOCK
    log_ok = functools.reduce(
        jnp.logical_or, [(lane == j) & (r >= d) for j, d in enumerate(dists)]
    )
    groups = rows // BLOCK
    for c in small_copies:
        c.wait()
    one_row = lax.broadcasted_iota(jnp.int32, (1, HEAD), 1) * 0
    chosen = [
        [
            [
                jnp.where(one_row + (p + d * groups - offsets[p, j]) == place, 1.0, 0.0)
                for place in range(groups)
            ]
            for j, d in enumerate(dists)
        ]
        for p in range(groups)
    ]
    chosen_low = [[[x.astype(bf16) for x in y] for y in z] for z in chosen]

    def block(x, p):
        return x[p * BLOCK:(p + 1) * BLOCK]

    def send_far(i):
        @pl.when(r >= 4)
        def _():
            g4_down(i).start()

        for n in range(len(far)):

            @pl.when(r >= far[n])
            def _(n=n):
                gfar_down(n, i).start()

    def send_near(i):
        @pl.when(r >= 1)
        def _():
            g1_mate(i).start()

    def compute(h):
        q = q_ref[h]
        do = do_ref[h]
        far_bufs = [rx2.at[h], rx4.at[h]] + [rxf.at[n, h] for n in range(len(far))]

        def picked(which):
            arrays = [buf[which] for buf in far_bufs[:len(dists)]]

            def pick(p, j):
                terms = [
                    block(arrays[j], place) * chosen_low[p][j][place] for place in range(groups)
                ]
                return functools.reduce(jnp.add, terms)

            return [
                jnp.concatenate([pick(p, j) for j in range(len(dists))], 0)
                for p in range(groups)
            ]

        arrive(2 * h)
        k_own, k_prev, k_log = own[h, 0], rx1[h, 0], picked(0)

        def against(x, a, b, log):
            near = jnp.where(tri, dot(x, a, NT), dot(x, b, NT))
            return near, jnp.concatenate(
                [dot(block(x, p), log[p], NT) for p in range(groups)], 0
            )

        def weighted(xa, xb, xl, a, b, log):
            return dot(xa, a, NN) + dot(xb, b, NN) + jnp.concatenate(
                [dot(block(xl, p), log[p], NN) for p in range(groups)], 0
            )

        w = window[h]
        limit = jnp.where(r >= 1, rows - w, 2 * rows)
        ok_win = (tri & (diff > -w)) | (diff > limit)
        s_win, s_log = against(q, k_own, k_prev, k_log)
        s_win = jnp.where(ok_win, s_win, NEG)
        s_log = jnp.where(log_ok, s_log, NEG)
        top = jnp.maximum(jnp.max(s_win, 1, keepdims=True), jnp.max(s_log, 1, keepdims=True))
        c = scale * math.log2(math.e)
        w_win = jnp.exp2((s_win - top) * c)
        w_log = jnp.exp2((s_log - top) * c)
        inv = 1.0 / (jnp.sum(w_win, 1, keepdims=True) + jnp.sum(w_log, 1, keepdims=True))
        p_win = w_win * inv
        p_log = w_log * inv
        low = p_win.astype(bf16)
        low_own = low * tri_low[0]
        low_log = p_log.astype(bf16)
        def scattered(parts, j):
            pieces = [block(x, j) for x in parts]
            return jnp.concatenate(
                [
                    functools.reduce(
                        jnp.add, [pieces[p] * chosen[p][j][place] for p in range(groups)]
                    )
                    for place in range(groups)
                ],
                0,
            )

        def keep(which, near, log, x, factor):
            i = 2 * h + which
            parts = [dot(block(log, p), block(x, p), TN) for p in range(groups)]
            flip = near.T
            flip_own = flip * tri_low[1]
            tg1[h, which] = (dot(flip - flip_own, x, NN) * factor).astype(bf16)
            send_near(i)
            for n in range(len(far)):
                tgf[n, h, which] = (scattered(parts, 2 + n) * factor).astype(bf16)
            if len(dists) > 1:
                tg4[h, which] = (scattered(parts, 1) * factor).astype(bf16)
            send_far(i)
            hold2[h, which] = scattered(parts, 0) * factor
            acc[h, which] = dot(flip_own, x, NN) * factor

        keep(1, low, low_log, do, 1.0)
        yield
        arrive(2 * h + 1)
        v_own, v_prev, v_log = own[h, 1], rx1[h, 1], picked(1)
        att = weighted(low_own, low - low_own, low_log, v_own, v_prev, v_log).astype(bf16)
        staged[0, h] = att
        result(0, h).start()
        delta = jnp.sum(att.astype(f32) * do.astype(f32), 1, keepdims=True)
        d_win, d_log = against(do, v_own, v_prev, v_log)
        ds = (p_win * (d_win - delta)).astype(bf16)
        ds_own = ds * tri_low[0]
        ds_log = (p_log * (d_log - delta)).astype(bf16)
        keep(0, ds, ds_log, q, scale)
        gq = weighted(ds_own, ds - ds_own, ds_log, k_own, k_prev, k_log) * scale
        staged[1, h] = gq.astype(bf16)
        result(1, h).start()
        yield

    def combine(i):
        h, w = i // 2, i % 2

        @pl.when((r >= 2) & has_up)
        def _():
            g4_down(i).wait_recv()
            hold2[h, w] = hold2[h, w] + rg4[h, w].astype(f32)

        @pl.when(odd & (r >= 3))
        def _():
            g1_mate(i).wait_recv()
            hold2[h, w] = hold2[h, w] + rg1[h, w].astype(f32)

        @pl.when(r >= 2)
        def _():
            ts2[h, w] = hold2[h, w].astype(bf16)
            s2_down(i).start()

    def relay(i):
        @pl.when(r >= 2)
        def _():
            own_up(i).wait_recv()

        @pl.when(odd & (r >= 3))
        def _():
            prev_relay(i).start()

        @pl.when((r >= 2) & has_up)
        def _():
            relay_up(i).start()

        if i + AHEAD < pieces:
            start_own(i + AHEAD)

    def arrive(i):
        @pl.when(r >= 1)
        def _():
            prev_own(i).wait_recv()

        @pl.when(r >= 4)
        def _():
            relay_up(i).wait_recv()

        for n in range(len(far)):

            @pl.when(r >= far[n])
            def _(n=n):
                far_up(n, i).wait_recv()

    def finish(i):
        h, w = i // 2, i % 2

        @pl.when(even)
        def _():
            g1_mate(i).wait_recv()
            acc[h, w] = acc[h, w] + rg1[h, w].astype(f32)

        for n in range(len(far)):

            @pl.when(r + far[n] < size)
            def _(n=n):
                gfar_down(n, i).wait_recv()
                acc[h, w] = acc[h, w] + rgf[n, h, w].astype(f32)

        @pl.when(has_up)
        def _():
            s2_down(i).wait_recv()
            acc[h, w] = acc[h, w] + rs2[h, w].astype(f32)

        staged[2 + w, h] = acc[h, w].astype(bf16)
        result(2 + w, h).start()

    back = [i for h in range(heads) for i in (2 * h + 1, 2 * h)]
    steps = [compute(h) for h in range(heads)]
    for i in range(AHEAD):
        relay(i)
    done = 0
    for i in range(pieces):
        next(steps[i // 2])
        if i + AHEAD < pieces:
            relay(i + AHEAD)
        due = i - LAG + (i >= pieces - 2)
        while done <= due:
            combine(back[done])
            done += 1
    for i in back[done:]:
        combine(i)
    for i in back:
        finish(i)

    for i in range(pieces):

        @pl.when(has_up)
        def _(i=i):
            own_up(i).wait_send()

        @pl.when((r >= 2) & has_up)
        def _(i=i):
            relay_up(i).wait_send()

        @pl.when(even | (r >= 3))
        def _(i=i):
            prev_own(i).wait_send()

        @pl.when(r >= 4)
        def _(i=i):
            g4_down(i).wait_send()

        @pl.when(r >= 2)
        def _(i=i):
            s2_down(i).wait_send()

        @pl.when(r >= 1)
        def _(i=i):
            g1_mate(i).wait_send()

        for n in range(len(far)):

            @pl.when(r + far[n] < size)
            def _(n=n, i=i):
                far_up(n, i).wait_send()

            @pl.when(r >= far[n])
            def _(n=n, i=i):
                gfar_down(n, i).wait_send()

    for n in range(4):
        for h in range(heads):
            result(n, h).wait()


def copy_out(*refs):
    ins, outs, (held, into, back) = refs[:4], refs[4:8], refs[8:]
    first = [pltpu.make_async_copy(ins[n], held.at[n], into.at[n]) for n in range(4)]
    second = [pltpu.make_async_copy(held.at[n], outs[n], back.at[n]) for n in range(4)]
    for c in first:
        c.start()
    for n in range(4):
        first[n].wait()
        second[n].start()
    for c in second:
        c.wait()


def on_device(queries, keys, values, grad_out, window, offsets):
    size = lax.axis_size("ctx")
    rows, feat = queries.shape
    heads = feat // HEAD
    far = tuple(2 ** (j + 1) for j in range(2, LEVELS) if 2 ** (j + 1) < size)
    nf = max(len(far), 1)
    kinds = 6 + 2 * len(far)
    hbm = pl.BlockSpec(memory_space=pltpu.HBM)
    pack = (heads, 2, rows, HEAD)
    small = pltpu.VMEM(pack, jnp.bfloat16)
    wide = pltpu.VMEM(pack, jnp.float32)
    more = pltpu.VMEM((nf,) + (pack if far else (1, 2, 16, HEAD)), jnp.bfloat16)
    out = jax.ShapeDtypeStruct((rows, feat), jnp.bfloat16)
    parts = pl.pallas_call(
        functools.partial(kernel, size, heads, far),
        out_shape=(out,) * 4,
        in_specs=[hbm] * 6,
        out_specs=(hbm,) * 4,
        scratch_shapes=[
            pltpu.VMEM((4, heads, rows, HEAD), jnp.bfloat16),
            pltpu.SMEM(window.shape, jnp.int32),
            pltpu.SMEM(offsets.shape, jnp.int32),
            pltpu.VMEM((heads, rows, HEAD), jnp.bfloat16),
            pltpu.VMEM((heads, rows, HEAD), jnp.bfloat16),
            pltpu.VMEM((2, rows, rows), jnp.bfloat16),
        ]
        + [small] * 4 + [more] + [small] * 3 + [more] + [small] * 3 + [more]
        + [wide] * 2
        + [pltpu.SemaphoreType.DMA((kinds, 2 * heads)), pltpu.SemaphoreType.DMA((kinds, 2 * heads))]
        + [pltpu.SemaphoreType.DMA((heads, 4)), pltpu.SemaphoreType.DMA((2,))]
        + [pltpu.SemaphoreType.DMA((4, heads))],
        compiler_params=pltpu.CompilerParams(
            collective_id=0, has_side_effects=True, vmem_limit_bytes=63 * 2**20
        ),
        cost_estimate=pl.CostEstimate(
            flops=12 * heads * rows * rows * HEAD * (4 + len(far)),
            bytes_accessed=16 * rows * feat,
            transcendentals=heads * rows * rows * (3 + len(far)),
        ),
    )(window, offsets, queries, keys, values, grad_out)
    return pl.pallas_call(
        copy_out,
        out_shape=(out,) * 4,
        in_specs=[hbm] * 4,
        out_specs=(hbm,) * 4,
        scratch_shapes=[
            pltpu.VMEM((4, rows, feat), jnp.bfloat16),
            pltpu.SemaphoreType.DMA((4,)),
            pltpu.SemaphoreType.DMA((4,)),
        ],
        compiler_params=pltpu.CompilerParams(vmem_limit_bytes=63 * 2**20),
        cost_estimate=pl.CostEstimate(
            flops=0, bytes_accessed=16 * rows * feat, transcendentals=0
        ),
    )(*parts)


def solution(mesh):
    cut = P(("dp", "ctx"), None)
    return jax.shard_map(
        on_device,
        mesh=mesh,
        in_specs=(cut, cut, cut, cut, P(), cut),
        out_specs=(cut,) * 4,
        check_vma=False,
    )
```

```python
import functools
import math

import jax
import jax.numpy as jnp
from jax import lax
from jax.experimental import pallas as pl
from jax.experimental.pallas import tpu as pltpu
from jax.sharding import PartitionSpec as P

BLOCK = 64
LEVELS = 4
HEAD = 128
NEG = -1e30
AHEAD = 2
LAG = 2
MESH = pl.DeviceIdType.MESH
NT = (((1,), (1,)), ((), ()))
TN = (((0,), (0,)), ((), ()))
NN = (((1,), (0,)), ((), ()))


def dot(a, b, dims):
    return lax.dot_general(a, b, dims, preferred_element_type=jnp.float32)


def kernel(
    size, heads, far,
    window_hbm, offsets_hbm, q_hbm, k_hbm, v_hbm, do_hbm,
    att_hbm, gq_hbm, gk_hbm, gv_hbm,
    staged, window, offsets, q_ref, do_ref, tri_low, own, rx1, rx2, rx4, rxf,
    tg1, tg4, ts2, tgf, rg1, rg4, rs2, rgd, rgf, hold2, acc,
    send, recv, load, load_small, store,
):
    f32, bf16 = jnp.float32, jnp.bfloat16
    rows = q_hbm.shape[0]
    r = lax.axis_index("ctx")
    odd = lax.rem(r, 2) == 1
    even = jnp.logical_not(odd)
    has_up = r + 2 < size
    direct = lax.rem(r // 2, 2) == 0
    passes = direct & (r >= 2) & has_up
    has_up4 = direct & (r + 4 < size)
    has_down4 = direct & (r >= 4)
    via = jnp.logical_not(direct) & (r >= 4)
    scale = HEAD ** -0.5
    mate = r + 1 - 2 * lax.rem(r, 2)

    K_OWN, K_REL, K_PRV, K_G4, K_S2, K_G1, K_FAR = 0, 1, 2, 3, 4, 5, 6
    K_GFAR = K_FAR + len(far)
    K_DIR = K_GFAR + len(far)
    K_GDIR = K_DIR + 1

    def copy(kind, h, src, dst, to):
        return pltpu.make_async_remote_copy(
            src_ref=src, dst_ref=dst, send_sem=send.at[kind, h], recv_sem=recv.at[kind, h],
            device_id={"ctx": to}, device_id_type=MESH,
        )

    def piece(buf, i):
        return buf.at[i // 2, i % 2]

    def own_up(i):
        return copy(K_OWN, i, piece(own, i), piece(rx2, i), r + 2)

    def relay_up(i):
        return copy(K_REL, i, piece(rx2, i), piece(rx4, i), r + 2)

    def direct_up(i):
        return copy(K_DIR, i, piece(own, i), piece(rx4, i), r + 4)

    def direct_down(i):
        return copy(K_GDIR, i, piece(tg4, i), piece(rgd, i), r - 4)

    def prev_own(i):
        return copy(K_PRV, i, piece(own, i), piece(rx1, i), mate)

    def prev_relay(i):
        return copy(K_PRV, i, piece(rx2, i), piece(rx1, i), mate)

    def far_up(n, i):
        return copy(K_FAR + n, i, piece(own, i), piece(rxf.at[n], i), r + far[n])

    def g4_down(i):
        return copy(K_G4, i, piece(tg4, i), piece(rg4, i), r - 2)

    def s2_down(i):
        return copy(K_S2, i, piece(ts2, i), piece(rs2, i), r - 2)

    def g1_mate(i):
        return copy(K_G1, i, piece(tg1, i), piece(rg1, i), mate)

    def gfar_down(n, i):
        return copy(K_GFAR + n, i, piece(tgf.at[n], i), piece(rgf.at[n], i), r - far[n])

    def result(n, h):
        out = (att_hbm, gq_hbm, gk_hbm, gv_hbm)[n]
        return pltpu.make_async_copy(
            staged.at[n, h], out.at[:, h * HEAD:(h + 1) * HEAD], store.at[n, h]
        )

    loads = []
    for h in range(heads):
        cols = slice(h * HEAD, (h + 1) * HEAD)
        loads.append([
            pltpu.make_async_copy(src.at[:, cols], dst, load.at[h, n])
            for n, (src, dst) in enumerate((
                (k_hbm, own.at[h, 0]), (v_hbm, own.at[h, 1]),
                (q_hbm, q_ref.at[h]), (do_hbm, do_ref.at[h]),
            ))
        ])
    small_copies = [
        pltpu.make_async_copy(offsets_hbm, offsets, load_small.at[0]),
        pltpu.make_async_copy(window_hbm, window, load_small.at[1]),
    ]
    for pair in (slice(0, 2), slice(2, 4)):
        for group in loads:
            for c in group[pair]:
                c.start()
    for c in small_copies:
        c.start()

    barrier = pltpu.get_barrier_semaphore()
    pl.semaphore_signal(barrier, inc=1, device_id={"ctx": mate}, device_id_type=MESH)
    count = 1
    for d in (2, 4) + far:
        for to, ok in ((r + d, r + d < size), (r - d, r >= d)):
            count = count + ok.astype(jnp.int32)

            @pl.when(ok)
            def _(to=to):
                pl.semaphore_signal(barrier, inc=1, device_id={"ctx": to}, device_id_type=MESH)

    for d, buf in ((1, rx1), (2, rx2), (4, rx4)):

        @pl.when(r < d)
        def _(buf=buf):
            buf[...] = jnp.zeros_like(buf)

    for n, d in enumerate(far):

        @pl.when(r < d)
        def _(n=n):
            rxf[n] = jnp.zeros(rxf.shape[1:], bf16)

    pl.semaphore_wait(barrier, count)

    pieces = 2 * heads

    def start_own(i):
        loads[i // 2][i % 2].wait()

        @pl.when(even)
        def _():
            prev_own(i).start()

        @pl.when(has_up)
        def _():
            own_up(i).start()

        @pl.when(has_up4)
        def _():
            direct_up(i).start()

        for n in range(len(far)):

            @pl.when(r + far[n] < size)
            def _(n=n):
                far_up(n, i).start()

    for i in range(AHEAD):
        start_own(i)
    for group in loads:
        for c in group[2:]:
            c.wait()

    query_i = lax.broadcasted_iota(jnp.int32, (rows, rows), 0)
    key_i = lax.broadcasted_iota(jnp.int32, (rows, rows), 1)
    diff = key_i - query_i
    tri = diff <= 0
    tri_low[0] = jnp.where(tri, 1.0, 0.0).astype(bf16)
    tri_low[1] = jnp.where(diff >= 0, 1.0, 0.0).astype(bf16)
    dists = (2, 4) + far
    wide_log = len(dists) * BLOCK
    lane = lax.broadcasted_iota(jnp.int32, (1, wide_log), 1) // BLOCK
    log_ok = functools.reduce(
        jnp.logical_or, [(lane == j) & (r >= d) for j, d in enumerate(dists)]
    )
    groups = rows // BLOCK
    for c in small_copies:
        c.wait()
    one_row = lax.broadcasted_iota(jnp.int32, (1, HEAD), 1) * 0
    chosen = [
        [
            [
                jnp.where(one_row + (p + d * groups - offsets[p, j]) == place, 1.0, 0.0)
                for place in range(groups)
            ]
            for j, d in enumerate(dists)
        ]
        for p in range(groups)
    ]
    chosen_low = [[[x.astype(bf16) for x in y] for y in z] for z in chosen]

    def block(x, p):
        return x[p * BLOCK:(p + 1) * BLOCK]

    def send_far(i):
        @pl.when(via)
        def _():
            g4_down(i).start()

        @pl.when(has_down4)
        def _():
            direct_down(i).start()

        for n in range(len(far)):

            @pl.when(r >= far[n])
            def _(n=n):
                gfar_down(n, i).start()

    def send_near(i):
        @pl.when(r >= 1)
        def _():
            g1_mate(i).start()

    def compute(h):
        q = q_ref[h]
        do = do_ref[h]
        far_bufs = [rx2.at[h], rx4.at[h]] + [rxf.at[n, h] for n in range(len(far))]

        def picked(which):
            arrays = [buf[which] for buf in far_bufs[:len(dists)]]

            def pick(p, j):
                terms = [
                    block(arrays[j], place) * chosen_low[p][j][place] for place in range(groups)
                ]
                return functools.reduce(jnp.add, terms)

            return [
                jnp.concatenate([pick(p, j) for j in range(len(dists))], 0)
                for p in range(groups)
            ]

        arrive(2 * h)
        k_own, k_prev, k_log = own[h, 0], rx1[h, 0], picked(0)

        def against(x, a, b, log):
            near = jnp.where(tri, dot(x, a, NT), dot(x, b, NT))
            return near, jnp.concatenate(
                [dot(block(x, p), log[p], NT) for p in range(groups)], 0
            )

        def weighted(xa, xb, xl, a, b, log):
            return dot(xa, a, NN) + dot(xb, b, NN) + jnp.concatenate(
                [dot(block(xl, p), log[p], NN) for p in range(groups)], 0
            )

        w = window[h]
        limit = jnp.where(r >= 1, rows - w, 2 * rows)
        ok_win = (tri & (diff > -w)) | (diff > limit)
        s_win, s_log = against(q, k_own, k_prev, k_log)
        s_win = jnp.where(ok_win, s_win, NEG)
        s_log = jnp.where(log_ok, s_log, NEG)
        top = jnp.maximum(jnp.max(s_win, 1, keepdims=True), jnp.max(s_log, 1, keepdims=True))
        c = scale * math.log2(math.e)
        w_win = jnp.exp2((s_win - top) * c)
        w_log = jnp.exp2((s_log - top) * c)
        inv = 1.0 / (jnp.sum(w_win, 1, keepdims=True) + jnp.sum(w_log, 1, keepdims=True))
        p_win = w_win * inv
        p_log = w_log * inv
        low = p_win.astype(bf16)
        low_own = low * tri_low[0]
        low_log = p_log.astype(bf16)
        def scattered(parts, j):
            pieces = [block(x, j) for x in parts]
            return jnp.concatenate(
                [
                    functools.reduce(
                        jnp.add, [pieces[p] * chosen[p][j][place] for p in range(groups)]
                    )
                    for place in range(groups)
                ],
                0,
            )

        def keep(which, near, log, x, factor):
            i = 2 * h + which
            parts = [dot(block(log, p), block(x, p), TN) for p in range(groups)]
            flip = near.T
            flip_own = flip * tri_low[1]
            tg1[h, which] = (dot(flip - flip_own, x, NN) * factor).astype(bf16)
            send_near(i)
            for n in range(len(far)):
                tgf[n, h, which] = (scattered(parts, 2 + n) * factor).astype(bf16)
            if len(dists) > 1:
                tg4[h, which] = (scattered(parts, 1) * factor).astype(bf16)
            send_far(i)
            hold2[h, which] = scattered(parts, 0) * factor
            acc[h, which] = dot(flip_own, x, NN) * factor

        keep(1, low, low_log, do, 1.0)
        yield
        arrive(2 * h + 1)
        v_own, v_prev, v_log = own[h, 1], rx1[h, 1], picked(1)
        att = weighted(low_own, low - low_own, low_log, v_own, v_prev, v_log).astype(bf16)
        staged[0, h] = att
        result(0, h).start()
        delta = jnp.sum(att.astype(f32) * do.astype(f32), 1, keepdims=True)
        d_win, d_log = against(do, v_own, v_prev, v_log)
        ds = (p_win * (d_win - delta)).astype(bf16)
        ds_own = ds * tri_low[0]
        ds_log = (p_log * (d_log - delta)).astype(bf16)
        keep(0, ds, ds_log, q, scale)
        gq = weighted(ds_own, ds - ds_own, ds_log, k_own, k_prev, k_log) * scale
        staged[1, h] = gq.astype(bf16)
        result(1, h).start()
        yield

    def combine(i):
        h, w = i // 2, i % 2

        @pl.when(passes)
        def _():
            g4_down(i).wait_recv()
            hold2[h, w] = hold2[h, w] + rg4[h, w].astype(f32)

        @pl.when(odd & (r >= 3))
        def _():
            g1_mate(i).wait_recv()
            hold2[h, w] = hold2[h, w] + rg1[h, w].astype(f32)

        @pl.when(r >= 2)
        def _():
            ts2[h, w] = hold2[h, w].astype(bf16)
            s2_down(i).start()

    def relay(i):
        @pl.when(r >= 2)
        def _():
            own_up(i).wait_recv()

        @pl.when(odd & (r >= 3))
        def _():
            prev_relay(i).start()

        @pl.when(passes)
        def _():
            relay_up(i).start()

        if i + AHEAD < pieces:
            start_own(i + AHEAD)

    def arrive(i):
        @pl.when(r >= 1)
        def _():
            prev_own(i).wait_recv()

        @pl.when(via)
        def _():
            relay_up(i).wait_recv()

        @pl.when(has_down4)
        def _():
            direct_up(i).wait_recv()

        for n in range(len(far)):

            @pl.when(r >= far[n])
            def _(n=n):
                far_up(n, i).wait_recv()

    def finish(i):
        h, w = i // 2, i % 2

        @pl.when(even)
        def _():
            g1_mate(i).wait_recv()
            acc[h, w] = acc[h, w] + rg1[h, w].astype(f32)

        for n in range(len(far)):

            @pl.when(r + far[n] < size)
            def _(n=n):
                gfar_down(n, i).wait_recv()
                acc[h, w] = acc[h, w] + rgf[n, h, w].astype(f32)

        @pl.when(has_up4)
        def _():
            direct_down(i).wait_recv()
            acc[h, w] = acc[h, w] + rgd[h, w].astype(f32)

        @pl.when(has_up)
        def _():
            s2_down(i).wait_recv()
            acc[h, w] = acc[h, w] + rs2[h, w].astype(f32)

        staged[2 + w, h] = acc[h, w].astype(bf16)
        result(2 + w, h).start()

    back = [i for h in range(heads) for i in (2 * h + 1, 2 * h)]
    steps = [compute(h) for h in range(heads)]
    for i in range(AHEAD):
        relay(i)
    for i in range(pieces):
        next(steps[i // 2])
        if i + AHEAD < pieces:
            relay(i + AHEAD)
        if i >= LAG:
            combine(back[i - LAG])
    for i in back[-LAG:]:
        combine(i)
    for i in back:
        finish(i)

    for i in range(pieces):

        @pl.when(has_up)
        def _(i=i):
            own_up(i).wait_send()

        @pl.when(passes)
        def _(i=i):
            relay_up(i).wait_send()

        @pl.when(has_up4)
        def _(i=i):
            direct_up(i).wait_send()

        @pl.when(even | (r >= 3))
        def _(i=i):
            prev_own(i).wait_send()

        @pl.when(via)
        def _(i=i):
            g4_down(i).wait_send()

        @pl.when(has_down4)
        def _(i=i):
            direct_down(i).wait_send()

        @pl.when(r >= 2)
        def _(i=i):
            s2_down(i).wait_send()

        @pl.when(r >= 1)
        def _(i=i):
            g1_mate(i).wait_send()

        for n in range(len(far)):

            @pl.when(r + far[n] < size)
            def _(n=n, i=i):
                far_up(n, i).wait_send()

            @pl.when(r >= far[n])
            def _(n=n, i=i):
                gfar_down(n, i).wait_send()

    for n in range(4):
        for h in range(heads):
            result(n, h).wait()


def copy_out(*refs):
    ins, outs, (held, into, back) = refs[:4], refs[4:8], refs[8:]
    first = [pltpu.make_async_copy(ins[n], held.at[n], into.at[n]) for n in range(4)]
    second = [pltpu.make_async_copy(held.at[n], outs[n], back.at[n]) for n in range(4)]
    for c in first:
        c.start()
    for n in range(4):
        first[n].wait()
        second[n].start()
    for c in second:
        c.wait()


def on_device(queries, keys, values, grad_out, window, offsets):
    size = lax.axis_size("ctx")
    rows, feat = queries.shape
    heads = feat // HEAD
    far = tuple(2 ** (j + 1) for j in range(2, LEVELS) if 2 ** (j + 1) < size)
    nf = max(len(far), 1)
    kinds = 8 + 2 * len(far)
    hbm = pl.BlockSpec(memory_space=pltpu.HBM)
    pack = (heads, 2, rows, HEAD)
    small = pltpu.VMEM(pack, jnp.bfloat16)
    wide = pltpu.VMEM(pack, jnp.float32)
    more = pltpu.VMEM((nf,) + (pack if far else (1, 2, 16, HEAD)), jnp.bfloat16)
    out = jax.ShapeDtypeStruct((rows, feat), jnp.bfloat16)
    parts = pl.pallas_call(
        functools.partial(kernel, size, heads, far),
        out_shape=(out,) * 4,
        in_specs=[hbm] * 6,
        out_specs=(hbm,) * 4,
        scratch_shapes=[
            pltpu.VMEM((4, heads, rows, HEAD), jnp.bfloat16),
            pltpu.SMEM(window.shape, jnp.int32),
            pltpu.SMEM(offsets.shape, jnp.int32),
            pltpu.VMEM((heads, rows, HEAD), jnp.bfloat16),
            pltpu.VMEM((heads, rows, HEAD), jnp.bfloat16),
            pltpu.VMEM((2, rows, rows), jnp.bfloat16),
        ]
        + [small] * 4 + [more] + [small] * 3 + [more] + [small] * 4 + [more]
        + [wide] * 2
        + [pltpu.SemaphoreType.DMA((kinds, 2 * heads)), pltpu.SemaphoreType.DMA((kinds, 2 * heads))]
        + [pltpu.SemaphoreType.DMA((heads, 4)), pltpu.SemaphoreType.DMA((2,))]
        + [pltpu.SemaphoreType.DMA((4, heads))],
        compiler_params=pltpu.CompilerParams(
            collective_id=0, has_side_effects=True, vmem_limit_bytes=63 * 2**20
        ),
        cost_estimate=pl.CostEstimate(
            flops=12 * heads * rows * rows * HEAD * (4 + len(far)),
            bytes_accessed=16 * rows * feat,
            transcendentals=heads * rows * rows * (3 + len(far)),
        ),
    )(window, offsets, queries, keys, values, grad_out)
    return pl.pallas_call(
        copy_out,
        out_shape=(out,) * 4,
        in_specs=[hbm] * 4,
        out_specs=(hbm,) * 4,
        scratch_shapes=[
            pltpu.VMEM((4, rows, feat), jnp.bfloat16),
            pltpu.SemaphoreType.DMA((4,)),
            pltpu.SemaphoreType.DMA((4,)),
        ],
        compiler_params=pltpu.CompilerParams(vmem_limit_bytes=63 * 2**20),
        cost_estimate=pl.CostEstimate(
            flops=0, bytes_accessed=16 * rows * feat, transcendentals=0
        ),
    )(*parts)


def solution(mesh):
    cut = P(("dp", "ctx"), None)
    return jax.shard_map(
        on_device,
        mesh=mesh,
        in_specs=(cut, cut, cut, cut, P(), cut),
        out_specs=(cut,) * 4,
        check_vma=False,
    )
```

```python
import functools
import math

import jax
import jax.numpy as jnp
from jax import lax
from jax.experimental import pallas as pl
from jax.experimental.pallas import tpu as pltpu
from jax.sharding import PartitionSpec as P

BLOCK = 64
LEVELS = 4
HEAD = 128
NEG = -1e30
AHEAD = 2
LAG = 3
MESH = pl.DeviceIdType.MESH
NT = (((1,), (1,)), ((), ()))
TN = (((0,), (0,)), ((), ()))
NN = (((1,), (0,)), ((), ()))


def dot(a, b, dims):
    return lax.dot_general(a, b, dims, preferred_element_type=jnp.float32)


def kernel(
    size, heads, far,
    window_hbm, offsets_hbm, q_hbm, k_hbm, v_hbm, do_hbm,
    att_hbm, gq_hbm, gk_hbm, gv_hbm,
    staged, window, offsets, q_ref, do_ref, tri_low, own, rx1, rx2, rx4, rxf,
    tg1, tg4, ts2, tgf, rg1, rg4, rs2, rgf, hold2, acc,
    send, recv, load, load_small, store,
):
    f32, bf16 = jnp.float32, jnp.bfloat16
    rows = q_hbm.shape[0]
    r = lax.axis_index("ctx")
    odd = lax.rem(r, 2) == 1
    even = jnp.logical_not(odd)
    has_up = r + 2 < size
    scale = HEAD ** -0.5
    mate = r + 1 - 2 * lax.rem(r, 2)

    K_OWN, K_REL, K_PRV, K_G4, K_S2, K_G1, K_FAR = 0, 1, 2, 3, 4, 5, 6
    K_GFAR = K_FAR + len(far)

    def copy(kind, h, src, dst, to):
        return pltpu.make_async_remote_copy(
            src_ref=src, dst_ref=dst, send_sem=send.at[kind, h], recv_sem=recv.at[kind, h],
            device_id={"ctx": to}, device_id_type=MESH,
        )

    def piece(buf, i):
        return buf.at[i // 2, i % 2]

    def own_up(i):
        return copy(K_OWN, i, piece(own, i), piece(rx2, i), r + 2)

    def relay_up(i):
        return copy(K_REL, i, piece(rx2, i), piece(rx4, i), r + 2)

    def prev_own(i):
        return copy(K_PRV, i, piece(own, i), piece(rx1, i), mate)

    def prev_relay(i):
        return copy(K_PRV, i, piece(rx2, i), piece(rx1, i), mate)

    def far_up(n, i):
        return copy(K_FAR + n, i, piece(own, i), piece(rxf.at[n], i), r + far[n])

    def g4_down(i):
        return copy(K_G4, i, piece(tg4, i), piece(rg4, i), r - 2)

    def s2_down(i):
        return copy(K_S2, i, piece(ts2, i), piece(rs2, i), r - 2)

    def g1_mate(i):
        return copy(K_G1, i, piece(tg1, i), piece(rg1, i), mate)

    def gfar_down(n, i):
        return copy(K_GFAR + n, i, piece(tgf.at[n], i), piece(rgf.at[n], i), r - far[n])

    def result(n, h):
        out = (att_hbm, gq_hbm, gk_hbm, gv_hbm)[n]
        return pltpu.make_async_copy(
            staged.at[n, h], out.at[:, h * HEAD:(h + 1) * HEAD], store.at[n, h]
        )

    loads = []
    for h in range(heads):
        cols = slice(h * HEAD, (h + 1) * HEAD)
        loads.append([
            pltpu.make_async_copy(src.at[:, cols], dst, load.at[h, n])
            for n, (src, dst) in enumerate((
                (k_hbm, own.at[h, 0]), (v_hbm, own.at[h, 1]),
                (q_hbm, q_ref.at[h]), (do_hbm, do_ref.at[h]),
            ))
        ])
    small_copies = [
        pltpu.make_async_copy(offsets_hbm, offsets, load_small.at[0]),
        pltpu.make_async_copy(window_hbm, window, load_small.at[1]),
    ]
    for pair in (slice(0, 2), slice(2, 4)):
        for group in loads:
            for c in group[pair]:
                c.start()
    for c in small_copies:
        c.start()

    barrier = pltpu.get_barrier_semaphore()
    pl.semaphore_signal(barrier, inc=1, device_id={"ctx": mate}, device_id_type=MESH)
    count = 1
    for d in (2,) + far:
        for to, ok in ((r + d, r + d < size), (r - d, r >= d)):
            count = count + ok.astype(jnp.int32)

            @pl.when(ok)
            def _(to=to):
                pl.semaphore_signal(barrier, inc=1, device_id={"ctx": to}, device_id_type=MESH)

    for d, buf in ((1, rx1), (2, rx2), (4, rx4)):

        @pl.when(r < d)
        def _(buf=buf):
            buf[...] = jnp.zeros_like(buf)

    for n, d in enumerate(far):

        @pl.when(r < d)
        def _(n=n):
            rxf[n] = jnp.zeros(rxf.shape[1:], bf16)

    pl.semaphore_wait(barrier, count)

    pieces = 2 * heads

    def start_own(i):
        loads[i // 2][i % 2].wait()

        @pl.when(even)
        def _():
            prev_own(i).start()

        @pl.when(has_up)
        def _():
            own_up(i).start()

        for n in range(len(far)):

            @pl.when(r + far[n] < size)
            def _(n=n):
                far_up(n, i).start()

    for i in range(AHEAD):
        start_own(i)
    for group in loads:
        for c in group[2:]:
            c.wait()

    query_i = lax.broadcasted_iota(jnp.int32, (rows, rows), 0)
    key_i = lax.broadcasted_iota(jnp.int32, (rows, rows), 1)
    diff = key_i - query_i
    tri = diff <= 0
    tri_low[0] = jnp.where(tri, 1.0, 0.0).astype(bf16)
    tri_low[1] = jnp.where(diff >= 0, 1.0, 0.0).astype(bf16)
    dists = (2, 4) + far
    wide_log = len(dists) * BLOCK
    lane = lax.broadcasted_iota(jnp.int32, (1, wide_log), 1) // BLOCK
    log_ok = functools.reduce(
        jnp.logical_or, [(lane == j) & (r >= d) for j, d in enumerate(dists)]
    )
    groups = rows // BLOCK
    for c in small_copies:
        c.wait()
    one_row = lax.broadcasted_iota(jnp.int32, (1, HEAD), 1) * 0
    chosen = [
        [
            [
                jnp.where(one_row + (p + d * groups - offsets[p, j]) == place, 1.0, 0.0)
                for place in range(groups)
            ]
            for j, d in enumerate(dists)
        ]
        for p in range(groups)
    ]
    chosen_low = [[[x.astype(bf16) for x in y] for y in z] for z in chosen]

    def block(x, p):
        return x[p * BLOCK:(p + 1) * BLOCK]

    def send_far(i):
        @pl.when(r >= 4)
        def _():
            g4_down(i).start()

        for n in range(len(far)):

            @pl.when(r >= far[n])
            def _(n=n):
                gfar_down(n, i).start()

    def send_near(i):
        @pl.when(r >= 1)
        def _():
            g1_mate(i).start()

    def compute(h):
        q = q_ref[h]
        do = do_ref[h]
        far_bufs = [rx2.at[h], rx4.at[h]] + [rxf.at[n, h] for n in range(len(far))]

        def picked(which):
            arrays = [buf[which] for buf in far_bufs[:len(dists)]]

            def pick(p, j):
                terms = [
                    block(arrays[j], place) * chosen_low[p][j][place] for place in range(groups)
                ]
                return functools.reduce(jnp.add, terms)

            return [
                jnp.concatenate([pick(p, j) for j in range(len(dists))], 0)
                for p in range(groups)
            ]

        arrive(2 * h)
        k_own, k_prev, k_log = own[h, 0], rx1[h, 0], picked(0)

        def against(x, a, b, log):
            near = jnp.where(tri, dot(x, a, NT), dot(x, b, NT))
            return near, jnp.concatenate(
                [dot(block(x, p), log[p], NT) for p in range(groups)], 0
            )

        def weighted(xa, xb, xl, a, b, log):
            return dot(xa, a, NN) + dot(xb, b, NN) + jnp.concatenate(
                [dot(block(xl, p), log[p], NN) for p in range(groups)], 0
            )

        w = window[h]
        limit = jnp.where(r >= 1, rows - w, 2 * rows)
        ok_win = (tri & (diff > -w)) | (diff > limit)
        s_win, s_log = against(q, k_own, k_prev, k_log)
        s_win = jnp.where(ok_win, s_win, NEG)
        s_log = jnp.where(log_ok, s_log, NEG)
        top = jnp.maximum(jnp.max(s_win, 1, keepdims=True), jnp.max(s_log, 1, keepdims=True))
        c = scale * math.log2(math.e)
        w_win = jnp.exp2((s_win - top) * c)
        w_log = jnp.exp2((s_log - top) * c)
        inv = 1.0 / (jnp.sum(w_win, 1, keepdims=True) + jnp.sum(w_log, 1, keepdims=True))
        p_win = w_win * inv
        p_log = w_log * inv
        low = p_win.astype(bf16)
        low_own = low * tri_low[0]
        low_log = p_log.astype(bf16)
        def scattered(parts, j):
            pieces = [block(x, j) for x in parts]
            return jnp.concatenate(
                [
                    functools.reduce(
                        jnp.add, [pieces[p] * chosen[p][j][place] for p in range(groups)]
                    )
                    for place in range(groups)
                ],
                0,
            )

        def keep(which, near, log, x, factor):
            i = 2 * h + which
            parts = [dot(block(log, p), block(x, p), TN) for p in range(groups)]
            flip = near.T
            flip_own = flip * tri_low[1]
            tg1[h, which] = (dot(flip - flip_own, x, NN) * factor).astype(bf16)
            send_near(i)
            for n in range(len(far)):
                tgf[n, h, which] = (scattered(parts, 2 + n) * factor).astype(bf16)
            if len(dists) > 1:
                tg4[h, which] = (scattered(parts, 1) * factor).astype(bf16)
            send_far(i)
            hold2[h, which] = scattered(parts, 0) * factor
            acc[h, which] = dot(flip_own, x, NN) * factor

        keep(1, low, low_log, do, 1.0)
        yield
        arrive(2 * h + 1)
        v_own, v_prev, v_log = own[h, 1], rx1[h, 1], picked(1)
        att = weighted(low_own, low - low_own, low_log, v_own, v_prev, v_log).astype(bf16)
        staged[0, h] = att
        result(0, h).start()
        delta = jnp.sum(att.astype(f32) * do.astype(f32), 1, keepdims=True)
        d_win, d_log = against(do, v_own, v_prev, v_log)
        ds = (p_win * (d_win - delta)).astype(bf16)
        ds_own = ds * tri_low[0]
        ds_log = (p_log * (d_log - delta)).astype(bf16)
        keep(0, ds, ds_log, q, scale)
        gq = weighted(ds_own, ds - ds_own, ds_log, k_own, k_prev, k_log) * scale
        staged[1, h] = gq.astype(bf16)
        result(1, h).start()
        yield

    def combine(i):
        h, w = i // 2, i % 2

        @pl.when((r >= 2) & has_up)
        def _():
            g4_down(i).wait_recv()
            hold2[h, w] = hold2[h, w] + rg4[h, w].astype(f32)

        @pl.when(odd & (r >= 3))
        def _():
            g1_mate(i).wait_recv()
            hold2[h, w] = hold2[h, w] + rg1[h, w].astype(f32)

        @pl.when(r >= 2)
        def _():
            ts2[h, w] = hold2[h, w].astype(bf16)
            s2_down(i).start()

    def relay(i):
        @pl.when(r >= 2)
        def _():
            own_up(i).wait_recv()

        @pl.when(odd & (r >= 3))
        def _():
            prev_relay(i).start()

        @pl.when((r >= 2) & has_up)
        def _():
            relay_up(i).start()

        if i + AHEAD < pieces:
            start_own(i + AHEAD)

    def arrive(i):
        @pl.when(r >= 1)
        def _():
            prev_own(i).wait_recv()

        @pl.when(r >= 4)
        def _():
            relay_up(i).wait_recv()

        for n in range(len(far)):

            @pl.when(r >= far[n])
            def _(n=n):
                far_up(n, i).wait_recv()

    def finish(i):
        h, w = i // 2, i % 2

        @pl.when(even)
        def _():
            g1_mate(i).wait_recv()
            acc[h, w] = acc[h, w] + rg1[h, w].astype(f32)

        for n in range(len(far)):

            @pl.when(r + far[n] < size)
            def _(n=n):
                gfar_down(n, i).wait_recv()
                acc[h, w] = acc[h, w] + rgf[n, h, w].astype(f32)

        @pl.when(has_up)
        def _():
            s2_down(i).wait_recv()
            acc[h, w] = acc[h, w] + rs2[h, w].astype(f32)

        staged[2 + w, h] = acc[h, w].astype(bf16)
        result(2 + w, h).start()

    back = [i for h in range(heads) for i in (2 * h + 1, 2 * h)]
    steps = [compute(h) for h in range(heads)]
    for i in range(AHEAD):
        relay(i)
    for i in range(pieces):
        next(steps[i // 2])
        if i + AHEAD < pieces:
            relay(i + AHEAD)
        if i >= LAG:
            combine(back[i - LAG])
    for i in back[-LAG:]:
        combine(i)
    for i in back:
        finish(i)

    for i in range(pieces):

        @pl.when(has_up)
        def _(i=i):
            own_up(i).wait_send()

        @pl.when((r >= 2) & has_up)
        def _(i=i):
            relay_up(i).wait_send()

        @pl.when(even | (r >= 3))
        def _(i=i):
            prev_own(i).wait_send()

        @pl.when(r >= 4)
        def _(i=i):
            g4_down(i).wait_send()

        @pl.when(r >= 2)
        def _(i=i):
            s2_down(i).wait_send()

        @pl.when(r >= 1)
        def _(i=i):
            g1_mate(i).wait_send()

        for n in range(len(far)):

            @pl.when(r + far[n] < size)
            def _(n=n, i=i):
                far_up(n, i).wait_send()

            @pl.when(r >= far[n])
            def _(n=n, i=i):
                gfar_down(n, i).wait_send()

    for n in range(4):
        for h in range(heads):
            result(n, h).wait()


def copy_out(*refs):
    ins, outs, (held, into, back) = refs[:4], refs[4:8], refs[8:]
    first = [pltpu.make_async_copy(ins[n], held.at[n], into.at[n]) for n in range(4)]
    second = [pltpu.make_async_copy(held.at[n], outs[n], back.at[n]) for n in range(4)]
    for c in first:
        c.start()
    for n in range(4):
        first[n].wait()
        second[n].start()
    for c in second:
        c.wait()


def on_device(queries, keys, values, grad_out, window, offsets):
    size = lax.axis_size("ctx")
    rows, feat = queries.shape
    heads = feat // HEAD
    far = tuple(2 ** (j + 1) for j in range(2, LEVELS) if 2 ** (j + 1) < size)
    nf = max(len(far), 1)
    kinds = 6 + 2 * len(far)
    hbm = pl.BlockSpec(memory_space=pltpu.HBM)
    pack = (heads, 2, rows, HEAD)
    small = pltpu.VMEM(pack, jnp.bfloat16)
    wide = pltpu.VMEM(pack, jnp.float32)
    more = pltpu.VMEM((nf,) + (pack if far else (1, 2, 16, HEAD)), jnp.bfloat16)
    out = jax.ShapeDtypeStruct((rows, feat), jnp.bfloat16)
    parts = pl.pallas_call(
        functools.partial(kernel, size, heads, far),
        out_shape=(out,) * 4,
        in_specs=[hbm] * 6,
        out_specs=(hbm,) * 4,
        scratch_shapes=[
            pltpu.VMEM((4, heads, rows, HEAD), jnp.bfloat16),
            pltpu.SMEM(window.shape, jnp.int32),
            pltpu.SMEM(offsets.shape, jnp.int32),
            pltpu.VMEM((heads, rows, HEAD), jnp.bfloat16),
            pltpu.VMEM((heads, rows, HEAD), jnp.bfloat16),
            pltpu.VMEM((2, rows, rows), jnp.bfloat16),
        ]
        + [small] * 4 + [more] + [small] * 3 + [more] + [small] * 3 + [more]
        + [wide] * 2
        + [pltpu.SemaphoreType.DMA((kinds, 2 * heads)), pltpu.SemaphoreType.DMA((kinds, 2 * heads))]
        + [pltpu.SemaphoreType.DMA((heads, 4)), pltpu.SemaphoreType.DMA((2,))]
        + [pltpu.SemaphoreType.DMA((4, heads))],
        compiler_params=pltpu.CompilerParams(
            collective_id=0, has_side_effects=True, vmem_limit_bytes=63 * 2**20
        ),
        cost_estimate=pl.CostEstimate(
            flops=12 * heads * rows * rows * HEAD * (4 + len(far)),
            bytes_accessed=16 * rows * feat,
            transcendentals=heads * rows * rows * (3 + len(far)),
        ),
    )(window, offsets, queries, keys, values, grad_out)
    return pl.pallas_call(
        copy_out,
        out_shape=(out,) * 4,
        in_specs=[hbm] * 4,
        out_specs=(hbm,) * 4,
        scratch_shapes=[
            pltpu.VMEM((4, rows, feat), jnp.bfloat16),
            pltpu.SemaphoreType.DMA((4,)),
            pltpu.SemaphoreType.DMA((4,)),
        ],
        compiler_params=pltpu.CompilerParams(vmem_limit_bytes=63 * 2**20),
        cost_estimate=pl.CostEstimate(
            flops=0, bytes_accessed=16 * rows * feat, transcendentals=0
        ),
    )(*parts)


def solution(mesh):
    cut = P(("dp", "ctx"), None)
    return jax.shard_map(
        on_device,
        mesh=mesh,
        in_specs=(cut, cut, cut, cut, P(), cut),
        out_specs=(cut,) * 4,
        check_vma=False,
    )
```
